32 devices in a mesh: area: 4 (over y, core), scen: 8 (over z, x).
Axes of the slice: x: 2, y: 2, z: 4, core: 2. Of those that a mesh axis runs over, the one named last changes fastest.
Arguments:
- start_dispatch: float32 [24, 32, 35840], P(None, 'scen', 'area'), may hold values from -6 to 6
- multipliers: float32 [24, 32, 35840], P(None, 'scen', 'area'), may hold values from -6 to 6
- demand: float32 [24, 35840], P(None, 'area'), may hold values from -6 to 6
- load_factor: float32 [32], replicated, may hold values from 0.5 to 2
- node_ids: int32 [12, 32], P(None, 'scen'), may hold values from 0 to 31, as said below
- block_values: float32 [280, 2, 128, 128], P('area'), may hold values from -0.375 to 0.375
- block_cols: int32 [280, 2], P('area'), may hold values from 0 to 69, as said below
- send_block: int32 [4], P('area'), may hold values from 0 to 69
- tie_source: int32 [16], P('area'), may hold values from 0 to 3, as said below
- tie_row: int32 [16], P('area'), may hold values from 0 to 69
- tie_weight: float32 [16, 128, 128], P('area'), may hold values from -0.5 to 0.5
Outputs:
- dispatch: float32 [24, 32, 35840], P(None, 'scen', 'area')
- new_multipliers: float32 [24, 32, 35840], P(None, 'scen', 'area')
The draws below stay inside these ranges and needn't reach their ends.
Inputs may be any that keep to these rules, and one draw needn't show every extreme that they name: `node_ids`: two scenarios s and s2 carry the same label at section k exactly when s // g == s2 // g with g = max(32 // 2^k, 1); labels of different nodes at one section differ. `block_cols`: the first stored block of block row i of an area has column i; the 2 columns of a row are distinct. `tie_source`: the boundary block feeding a tie of area a belongs to area (a + 1) mod 4 or (a - 1) mod 4; every area receives from both.
All inputs are finite; a program needn't handle non-finite values.
Results may differ from the reference program's by a relative error of at most 0.0001.
Values sent between devices are 32-bit elements; how exact they have to be, the bound alone decides.
No kernel may reach another device: no remote copies, remote signals or barrier semaphores. Data moves between devices by JAX's collectives and lax.ppermute only.
A program may use at most 128 MiB of HBM per device.

```python
import math
import jax
import jax.numpy as jnp
from jax import lax

SECTIONS = 12
PER_SECTION = 2
T_PER = 24
SCEN = 32
BLK = 128
NBLK_DEV = 70
BUSES = 35840
NNZB = 2
NB = 1
MT = 4
STEPS = 8
N_AREA = 4


def draw_node_ids(key, part):
    scenario = jnp.arange(SCEN, dtype=jnp.int32)
    stacked = []
    for which_section in range(SECTIONS):
        members = max(SCEN >> which_section, 1)
        shuffled = jax.random.permutation(jax.random.fold_in(key, which_section), SCEN).astype(jnp.int32)
        stacked.append(shuffled[scenario // members])
    return jnp.stack(stacked).astype(jnp.int32)


def draw_block_cols(key, part):
    row_count = N_AREA * NBLK_DEV
    diagonal = jnp.arange(row_count, dtype=jnp.int32) % NBLK_DEV
    row_keys = jax.random.split(jax.random.fold_in(key, 7), row_count)

    def offsets_for(row_key):
        return jax.random.permutation(row_key, NBLK_DEV - 1)[:NNZB - 1].astype(jnp.int32)
    offsets = jax.vmap(offsets_for)(row_keys) + 1
    others = (diagonal[:, None] + offsets) % NBLK_DEV
    return jnp.concatenate([diagonal[:, None], others], axis=1).astype(jnp.int32)


def draw_tie_source(key, part):
    total = N_AREA * MT
    area_of = jnp.arange(total, dtype=jnp.int32) // MT
    within = jnp.arange(total, dtype=jnp.int32) % MT
    random_side = jax.random.randint(jax.random.fold_in(key, 3), (total,), 0, 2).astype(jnp.int32) * 2 - 1
    side = jnp.where(within == 0, 1, jnp.where(within == 1, -1, random_side))
    owners = (area_of + side + N_AREA) % N_AREA
    chosen = jax.random.randint(jax.random.fold_in(key, 5), (total,), 0, NB).astype(jnp.int32)
    return (owners * NB + chosen).astype(jnp.int32)


def place_ends(array, own_key, least, top_value):
    spot = [jax.random.randint(jax.random.fold_in(own_key, axis), (), 0, length) for axis, length in enumerate(array.shape)]
    main_axis = array.shape.index(max(array.shape))
    next_to = spot[:main_axis] + [(spot[main_axis] + 1) % array.shape[main_axis]] + spot[main_axis + 1:]
    return array.at[tuple(spot)].set(least).at[tuple(next_to)].set(top_value)


def steps_of(stream_key, extent, shards, smallest, largest):
    def one(dim, shards_of):
        steps = jax.random.uniform(jax.random.fold_in(jax.random.fold_in(stream_key, 6), dim), (shards_of,), jnp.float32, smallest / len(shards), largest / len(shards))
        return jnp.repeat(jnp.exp(steps), extent[dim] // shards_of).reshape((-1,) + (1,) * (len(extent) - dim - 1))

    loudness = one(*shards[0])
    for cut in shards[1:]:
        loudness = loudness * one(*cut)
    return loudness


def centred(key, shape, scale, most, shards=(), kind=jnp.bfloat16):
    loudness = steps_of(key, shape, shards, -0.22, 0.18) if shards else 1.0
    drawn = jax.random.normal(key, shape, jnp.float32) * scale * loudness
    return jnp.minimum(jnp.maximum(drawn, -most), most).astype(kind)


def setup_inputs(seed: int = 0) -> dict:
    arg_keys = jax.random.split(jax.random.key(seed), 12)
    return {
        "start_dispatch": centred(arg_keys[0], (T_PER, SCEN, BUSES), 1.0, 6.0, ((1, 8), (2, 4)), jnp.float32),
        "multipliers": centred(arg_keys[1], (T_PER, SCEN, BUSES), 1.0, 6.0, ((1, 8), (2, 4)), jnp.float32),
        "demand": centred(arg_keys[2], (T_PER, BUSES), 1.0, 6.0, ((1, 4),), jnp.float32),
        "load_factor": jnp.clip(jnp.exp(jax.random.uniform(arg_keys[3], (SCEN,), jnp.float32, math.log(0.5), math.log(2.0))), 0.5, 2.0),
        "node_ids": draw_node_ids(jax.random.fold_in(arg_keys[11], 71), 0),
        "block_values": centred(arg_keys[5], (NBLK_DEV * N_AREA, NNZB, BLK, BLK), (BLK * NNZB) ** -0.5, 0.375, ((0, 4),), jnp.float32),
        "block_cols": draw_block_cols(jax.random.fold_in(arg_keys[11], 71), 0),
        "send_block": place_ends(jax.random.randint(arg_keys[7], (NB * N_AREA,), 0, NBLK_DEV), jax.random.fold_in(arg_keys[7], 1), 0, NBLK_DEV - 1).astype(jnp.int32),
        "tie_source": draw_tie_source(jax.random.fold_in(arg_keys[11], 71), 0),
        "tie_row": place_ends(jax.random.randint(arg_keys[9], (MT * N_AREA,), 0, NBLK_DEV), jax.random.fold_in(arg_keys[9], 1), 0, NBLK_DEV - 1).astype(jnp.int32),
        "tie_weight": centred(arg_keys[10], (MT * N_AREA, BLK, BLK), BLK ** -0.5, 0.5, ((0, 4),), jnp.float32),
    }


full_precision = lax.Precision.HIGHEST
step_size = 0.25
penalty = 1.0


def average(values_in, node_ids):
    repeated = jnp.repeat(node_ids, PER_SECTION, axis=0)

    def period_average(packed):
        period_values, period_ids = packed
        sums = jax.ops.segment_sum(period_values, period_ids, num_segments=SCEN)
        counts = jax.ops.segment_sum(jnp.ones((SCEN,), period_values.dtype), period_ids, num_segments=SCEN)
        return sums[period_ids] / counts[period_ids][:, None]

    return lax.map(period_average, (values_in, repeated))


def operator_period(period_values, block_values, block_cols, send_block, tie_source, tie_row, tie_weight):
    blocks_all = BUSES // BLK
    shaped = period_values.reshape(SCEN, blocks_all, BLK)
    offsets = (jnp.arange(blocks_all, dtype=jnp.int32) // NBLK_DEV) * NBLK_DEV
    columns = block_cols + offsets[:, None]
    pieces = shaped[:, columns]
    product = jnp.einsum("sbjc,bjcd->sbd", pieces, block_values, precision=full_precision)
    owners = tie_source // NB
    sources = owners * NBLK_DEV + send_block[tie_source]
    targets = (jnp.arange(N_AREA * MT, dtype=jnp.int32) // MT) * NBLK_DEV + tie_row
    coupled = jnp.einsum("smc,mcd->smd", shaped[:, sources], tie_weight, precision=full_precision)
    product = product.at[:, targets].add(coupled)
    return product.reshape(SCEN, BUSES)


def reference(start_dispatch, multipliers, demand, load_factor, node_ids, block_values, block_cols, send_block, tie_source, tie_row, tie_weight):
    load_rows = jnp.repeat(load_factor[node_ids], PER_SECTION, axis=0)
    target = demand[:, None, :] * load_rows[:, :, None]
    anchor = average(start_dispatch, node_ids)
    dispatch = start_dispatch

    def apply_once(period_values):
        return operator_period(period_values, block_values, block_cols, send_block, tie_source, tie_row, tie_weight)

    for iteration in range(STEPS):
        product = lax.map(apply_once, dispatch)
        dispatch = dispatch - step_size * (product + multipliers - target + penalty * (dispatch - anchor))
    current = average(dispatch, node_ids)
    return dispatch, multipliers + penalty * (dispatch - current)
```

```python
import functools

import jax
import jax.numpy as jnp
from jax import lax
from jax.experimental import pallas as pl
from jax.experimental.pallas import tpu as pltpu
from jax.sharding import PartitionSpec as P

STEPS = 8
step_size = 0.25
penalty = 1.0
keep = 1.0 - step_size * penalty

f32 = jnp.float32
bf16 = jnp.bfloat16
VMEM = pltpu.VMEM
SMEM = pltpu.SMEM
MIB = 1 << 20


def in_vmem(array):
    return pltpu.with_memory_space_constraint(array, VMEM)


def in_smem(array):
    return pltpu.with_memory_space_constraint(array, SMEM)


def in_hbm(array):
    return pltpu.with_memory_space_constraint(array, pltpu.HBM)


vmem_spec = pl.BlockSpec(memory_space=VMEM)
smem_spec = pl.BlockSpec(memory_space=SMEM)
any_spec = pl.BlockSpec(memory_space=pl.ANY)


def params(mib):
    return pltpu.CompilerParams(vmem_limit_bytes=mib * MIB)


def cost(flops, moved):
    return pl.CostEstimate(flops=flops, bytes_accessed=moved, transcendentals=0)


def split(value):
    high = value.astype(bf16)
    return high, (value - high.astype(f32)).astype(bf16)


def store_split(ref, index, value):
    rows = value.shape[0]
    high, low = split(value)
    ref[index, 0:rows] = high
    ref[index, rows : 2 * rows] = low


def fold(product, rows):
    return (product[:rows, :128] + product[:rows, 128:]) + (product[rows:, :128] + product[rows:, 128:])


def lanes(block):
    return pl.ds(pl.multiple_of(block * 128, 128), 128)


def partner(value, apart):
    rows = value.shape[0]
    up = pltpu.roll(value, rows - apart, 0)
    down = pltpu.roll(value, apart, 0)
    place = lax.broadcasted_iota(jnp.int32, value.shape, 0)
    return jnp.where((place & apart) == 0, up, down)


def local_mean(value, members):
    total, apart = value, 1
    while apart < members:
        total = total + partner(total, apart)
        apart *= 2
    return total / members


def spread(pair, scenarios):
    count, width = pair.shape
    wide = jnp.broadcast_to(pair[:, None, :], (count, scenarios, width))
    return wide.reshape(count * scenarios, width)


def first_kernel(shared, per, cols, send, tie_row, start, *refs):
    sums, boundary = refs[:shared], refs[shared]
    cols_out, send_out, row_out = refs[shared + 1 : shared + 4]
    head, block, sems = refs[shared + 4 :]
    copy_head = pltpu.make_async_copy(start.at[0 : shared * per], head, sems.at[0])
    copy_block = pltpu.make_async_copy(start.at[:, :, lanes(send[0])], block, sems.at[1])
    copy_head.start()
    copy_block.start()

    def move(i, carry):
        cols_out[i] = cols[i]
        return carry

    lax.fori_loop(0, cols.shape[0], move, 0)
    send_out[0] = send[0]
    for m in range(tie_row.shape[0]):
        row_out[m] = tie_row[m]
    copy_block.wait()
    boundary[...] = block[...].reshape(boundary.shape)
    copy_head.wait()
    for k in range(shared):
        sums[k][...] = jnp.sum(head[k * per : (k + 1) * per], axis=1)


def add_kernel(count, *refs):
    for k in range(count):
        refs[2 * count + k][...] = refs[k][...] + refs[count + k][...]


def node_totals(sums):
    shared = len(sums)
    totals = list(sums)
    for turn in range(shared):
        active = [k for k in range(shared) if shared - k - 1 - turn >= 0]
        received = [swap(totals[k], "scen", shared - k - 1 - turn) for k in active]
        added = pl.pallas_call(
            functools.partial(add_kernel, len(active)),
            in_specs=[vmem_spec] * (2 * len(active)),
            out_specs=[vmem_spec] * len(active),
            out_shape=[VMEM(totals[k].shape, f32) for k in active],
            compiler_params=params(2),
            name=f"node_add_{turn}",
        )(*[in_vmem(totals[k]) for k in active], *[in_vmem(r) for r in received])
        for k, value in zip(active, added):
            totals[k] = value
    return totals


def swap(block, axis, level):
    count = lax.axis_size(axis)
    return lax.ppermute(block, axis, [(i, i ^ (1 << level)) for i in range(count)])


def from_behind(value, axis, by):
    count = lax.axis_size(axis)
    return lax.ppermute(value, axis, [(i, (i + by) % count) for i in range(count)])


def prepare_kernel(shared, per, scen_all, chunk, side, values, start, mult, demand, load, tie_weight,
                   weights, ties, state, parts, constant):
    step = pl.program_id(0)
    rows = state.shape[1]
    scenarios = start.shape[1]
    group = per * scenarios

    def one(b, carry):
        i = step * chunk + b
        for j in range(2):
            high, low = split(values[b, j] * -step_size)
            weights[i, j * 128 : (j + 1) * 128, 0:128] = high
            weights[i, j * 128 : (j + 1) * 128, 128:256] = low
        x = start[:, :, lanes(b)].reshape(rows, 128)
        m = mult[:, :, lanes(b)].reshape(rows, 128)
        target = spread(demand[:, lanes(b)], scenarios) * load[...]
        state[i] = x
        store_split(parts, i, x)
        rest = m - target
        for k in range(rows // group):
            cut = slice(k * group, (k + 1) * group)
            piece = rest[cut]
            members = max(scen_all >> k, 1)
            if k >= shared:
                piece = piece - penalty * local_mean(x[cut], members)
            constant[i, cut] = -step_size * piece
        return carry

    lax.fori_loop(0, chunk, one, 0, unroll=True)

    @pl.when(step == 0)
    def _():
        for m in range(tie_weight.shape[0]):
            high, low = split(tie_weight[m] * -step_size)
            below = jnp.full((128, 128), side[m], jnp.int32) == 0
            zero = jnp.zeros((128, 128), f32)
            for n, part in enumerate((high.astype(f32), low.astype(f32))):
                cut = slice(n * 128, (n + 1) * 128)
                ties[m, 0:128, cut] = jnp.where(below, part, zero).astype(bf16)
                ties[m, 128:256, cut] = jnp.where(below, zero, part).astype(bf16)


def step_kernel(cols, weights, state, parts, constant, new_state, new_parts):
    rows = state.shape[1]
    for i in range(state.shape[0]):
        other = cols[2 * i + 1]
        left = jnp.concatenate([parts[i], parts[other]], axis=1)
        product = jnp.dot(left, weights[i], preferred_element_type=f32)
        value = (keep * state[i] + constant[i]) + fold(product, rows)
        new_state[i] = value
        store_split(new_parts, i, value)


def add_ties(tie_row, low, high, ties, state, parts):
    rows = state.shape[1]
    both = jnp.concatenate([low[...], high[...]], axis=1)
    left = jnp.concatenate(split(both), axis=0)
    for m in range(ties.shape[0]):
        added = fold(jnp.dot(left, ties[m], preferred_element_type=f32), rows)
        row = tie_row[m]
        state[row] = state[row] + added
    for m in range(ties.shape[0]):
        row = tie_row[m]
        store_split(parts, row, state[row])


def tie_kernel(tie_row, send, low, high, ties, state_in, parts_in, state, parts, boundary):
    add_ties(tie_row, low, high, ties, state, parts)
    boundary[...] = state[send[0]]


def anchor_kernel(shared, scen_all, scenarios, tie_row, send, low, high, ties, *refs):
    totals = refs[:shared]
    state, parts, constant, boundary = refs[shared + 3 :]
    rows = state.shape[1]
    group = totals[0].shape[0] * scenarios
    span = min(-(-shared * group // 16) * 16, rows)

    def one(i, carry):
        for k in range(shared):
            cut = slice(k * group, (k + 1) * group)
            mean = spread(totals[k][:, lanes(i)], scenarios) / (scen_all >> k)
            mean = (step_size * penalty) * mean
            constant[i, cut] = constant[i, cut] + mean
            state[i, cut] = state[i, cut] + mean
        high_part, low_part = split(state[i, 0:span])
        parts[i, 0:span] = high_part
        parts[i, rows : rows + span] = low_part
        return carry

    lax.fori_loop(0, state.shape[0], one, 0, unroll=7)
    add_ties(tie_row, low, high, ties, state, parts)
    boundary[...] = state[send[0]]


def last_tie_kernel(shared, per, scenarios, tie_row, low, high, ties, state_in, parts_in, state, *refs):
    sums, parts = refs[:shared], refs[shared]
    add_ties(tie_row, low, high, ties, state, parts)
    group = per * scenarios

    def one(i, carry):
        for k in range(shared):
            piece = state[i, k * group : (k + 1) * group].reshape(per, scenarios, 128)
            sums[k][:, lanes(i)] = jnp.sum(piece, axis=1)
        return carry

    lax.fori_loop(0, state.shape[0], one, 0, unroll=7)


def output_kernel(shared, per, scen_all, chunk, state, mult, dispatch, new_mult):
    step = pl.program_id(0)
    rows = state.shape[1]
    periods, scenarios = mult.shape[:2]
    group = per * scenarios

    def one(b, carry):
        value = state[step * chunk + b]
        dispatch[:, :, lanes(b)] = value.reshape(periods, scenarios, 128)
        m = mult[:, :, lanes(b)].reshape(rows, 128)
        for k in range(rows // group):
            cut = slice(k * group, (k + 1) * group)
            members = max(scen_all >> k, 1)
            piece = m[cut]
            if k >= shared:
                piece = piece + penalty * (value[cut] - local_mean(value[cut], members))
            new_mult[k * per : (k + 1) * per, :, lanes(b)] = piece.reshape(per, scenarios, 128)
        return carry

    lax.fori_loop(0, chunk, one, 0, unroll=True)


def finish_kernel(shared, per, scen_all, state, *refs):
    totals = refs[:shared]
    new_in, new_mult, buffer, sems = refs[shared:]
    periods, scenarios = buffer.shape[:2]
    group = per * scenarios
    fetch = pltpu.make_async_copy(new_mult.at[0:periods], buffer, sems.at[0])
    fetch.start()
    fetch.wait()

    def one(i, carry):
        for k in range(shared):
            value = state[i, k * group : (k + 1) * group]
            mean = spread(totals[k][:, lanes(i)], scenarios) / (scen_all >> k)
            gap = penalty * (value - mean)
            cut = slice(k * per, (k + 1) * per)
            buffer[cut, :, lanes(i)] = buffer[cut, :, lanes(i)] + gap.reshape(per, scenarios, 128)
        return carry

    lax.fori_loop(0, state.shape[0], one, 0, unroll=7)
    back = pltpu.make_async_copy(buffer, new_mult.at[0:periods], sems.at[0])
    back.start()
    back.wait()


def largest_divisor(count, most):
    return max(d for d in range(1, most + 1) if count % d == 0)


def local(
    start_dispatch,
    multipliers,
    demand,
    load_factor,
    node_ids,
    block_values,
    block_cols,
    send_block,
    tie_source,
    tie_row,
    tie_weight,
):
    periods, scenarios, buses = start_dispatch.shape
    blocks = buses // 128
    rows = periods * scenarios
    sections = node_ids.shape[0]
    per = periods // sections
    devices = lax.axis_size("scen")
    scen_all = scenarios * devices
    shared = devices.bit_length() - 1
    tie_count = tie_row.shape[0]
    chunk = largest_divisor(blocks, 7)

    labels = jnp.arange(load_factor.shape[0], dtype=jnp.int32)
    matches = node_ids[:, :, None] == labels[None, None, :]
    load_rows = jnp.sum(jnp.where(matches, load_factor[None, None, :], 0.0), axis=2)
    load_rows = jnp.repeat(load_rows, per, axis=0).reshape(rows, 1)
    load_wide = jnp.broadcast_to(load_rows, (rows, 128))
    before = (lax.axis_index("area") - 1 + lax.axis_size("area")) % lax.axis_size("area")
    side = jnp.where(tie_source // send_block.shape[0] == before, 0, 1)

    first = pl.pallas_call(
        functools.partial(first_kernel, shared, per),
        in_specs=[smem_spec] * 3 + [any_spec],
        out_specs=[vmem_spec] * (shared + 1) + [smem_spec] * 3,
        out_shape=[VMEM((per, buses), f32)] * shared
        + [VMEM((rows, 128), f32), SMEM((2 * blocks,), jnp.int32), SMEM((1,), jnp.int32), SMEM((tie_count,), jnp.int32)],
        scratch_shapes=[
            VMEM((shared * per, scenarios, buses), f32),
            VMEM((periods, scenarios, 128), f32),
            pltpu.SemaphoreType.DMA((2,)),
        ],
        compiler_params=params(6),
        name="first_sums",
    )(block_cols.reshape(-1), send_block, tie_row, in_hbm(start_dispatch))
    sums, boundary = list(first[:shared]), first[shared]
    cols, send, row_of_tie = first[shared + 1 :]

    weights, ties, state, parts, constant = pl.pallas_call(
        functools.partial(prepare_kernel, shared, per, scen_all, chunk),
        grid=(blocks // chunk,),
        in_specs=[
            smem_spec,
            pl.BlockSpec((chunk, 2, 128, 128), lambda i: (i, 0, 0, 0)),
            pl.BlockSpec((periods, scenarios, chunk * 128), lambda i: (0, 0, i)),
            pl.BlockSpec((periods, scenarios, chunk * 128), lambda i: (0, 0, i)),
            pl.BlockSpec((periods, chunk * 128), lambda i: (0, i)),
            vmem_spec,
            vmem_spec,
        ],
        out_specs=[vmem_spec] * 5,
        out_shape=[
            VMEM((blocks, 256, 256), bf16),
            VMEM((tie_count, 256, 256), bf16),
            VMEM((blocks, rows, 128), f32),
            VMEM((blocks, 2 * rows, 128), bf16),
            VMEM((blocks, rows, 128), f32),
        ],
        compiler_params=params(10),
        cost_estimate=cost(10**9, 20 * 10**6),
        name="prepare",
    )(side, in_hbm(block_values), in_hbm(start_dispatch), in_hbm(multipliers), in_hbm(demand), load_wide, tie_weight)

    state_shape = VMEM((blocks, rows, 128), f32)
    parts_shape = VMEM((blocks, 2 * rows, 128), bf16)

    totals = node_totals(sums)
    for iteration in range(STEPS):
        low = from_behind(boundary, "area", 1)
        high = from_behind(boundary, "area", -1)
        state, parts = pl.pallas_call(
            step_kernel,
            in_specs=[smem_spec] + [vmem_spec] * 4,
            out_specs=[vmem_spec] * 2,
            out_shape=[state_shape, parts_shape],
            compiler_params=params(2),
            cost_estimate=cost(blocks * 2 * rows * 256 * 256 * 2, 12 * 10**6),
            name=f"step_{iteration}",
        )(in_smem(cols), in_vmem(weights), in_vmem(state), in_vmem(parts), in_vmem(constant))
        tie_args = [in_vmem(low), in_vmem(high), in_vmem(ties)]
        if iteration == 0:
            state, parts, constant, boundary = pl.pallas_call(
                functools.partial(anchor_kernel, shared, scen_all, scenarios),
                in_specs=[smem_spec] * 2 + [vmem_spec] * (6 + shared),
                out_specs=[vmem_spec] * 4,
                out_shape=[state_shape, parts_shape, state_shape, VMEM((rows, 128), f32)],
                input_output_aliases={5 + shared: 0, 6 + shared: 1, 7 + shared: 2},
                compiler_params=params(2),
                name="anchor",
            )(in_smem(row_of_tie), in_smem(send), *tie_args, *[in_vmem(t) for t in totals],
              in_vmem(state), in_vmem(parts), in_vmem(constant))
        elif iteration < STEPS - 1:
            state, parts, boundary = pl.pallas_call(
                tie_kernel,
                in_specs=[smem_spec] * 2 + [vmem_spec] * 5,
                out_specs=[vmem_spec] * 3,
                out_shape=[state_shape, parts_shape, VMEM((rows, 128), f32)],
                input_output_aliases={5: 0, 6: 1},
                compiler_params=params(2),
                name=f"ties_{iteration}",
            )(in_smem(row_of_tie), in_smem(send), *tie_args, in_vmem(state), in_vmem(parts))
        else:
            last = pl.pallas_call(
                functools.partial(last_tie_kernel, shared, per, scenarios),
                in_specs=[smem_spec] + [vmem_spec] * 5,
                out_specs=[vmem_spec] * (2 + shared),
                out_shape=[state_shape] + [VMEM((per, buses), f32)] * shared + [parts_shape],
                input_output_aliases={4: 0, 5: 1 + shared},
                compiler_params=params(2),
                name=f"ties_{iteration}",
            )(in_smem(row_of_tie), *tie_args, in_vmem(state), in_vmem(parts))
            state, sums = last[0], list(last[1 : 1 + shared])

    totals = node_totals(sums)
    block = pl.BlockSpec((periods, scenarios, chunk * 128), lambda i: (0, 0, i))
    whole = jax.ShapeDtypeStruct((periods, scenarios, buses), f32)
    dispatch, new_mult = pl.pallas_call(
        functools.partial(output_kernel, shared, per, scen_all, chunk),
        grid=(blocks // chunk,),
        in_specs=[vmem_spec, block],
        out_specs=[block, block],
        out_shape=[whole, whole],
        compiler_params=params(10),
        cost_estimate=cost(10**9, 12 * 10**6),
        name="outputs",
    )(in_vmem(state), in_hbm(multipliers))
    new_mult = pl.pallas_call(
        functools.partial(finish_kernel, shared, per, scen_all),
        in_specs=[vmem_spec] * (1 + shared) + [any_spec],
        out_specs=any_spec,
        out_shape=whole,
        input_output_aliases={1 + shared: 0},
        scratch_shapes=[VMEM((shared * per, scenarios, buses), f32), pltpu.SemaphoreType.DMA((1,))],
        compiler_params=params(6),
        name="finish",
    )(in_vmem(state), *[in_vmem(t) for t in totals], in_hbm(new_mult))
    return dispatch, new_mult


def solution(mesh):
    in_specs = (
        P(None, "scen", "area"),
        P(None, "scen", "area"),
        P(None, "area"),
        P(),
        P(None, "scen"),
        P("area", None, None, None),
        P("area", None),
        P("area"),
        P("area"),
        P("area"),
        P("area", None, None),
    )
    out_specs = (P(None, "scen", "area"), P(None, "scen", "area"))
    return jax.shard_map(local, mesh=mesh, in_specs=in_specs, out_specs=out_specs, check_vma=False)
```

```python
import functools

import jax
import jax.numpy as jnp
from jax import lax
from jax.experimental import pallas as pl
from jax.experimental.pallas import tpu as pltpu
from jax.sharding import PartitionSpec as P

STEPS = 8
step_size = 0.25
penalty = 1.0
keep = 1.0 - step_size * penalty

f32 = jnp.float32
bf16 = jnp.bfloat16
VMEM = pltpu.VMEM
SMEM = pltpu.SMEM
MIB = 1 << 20


def in_vmem(array):
    return pltpu.with_memory_space_constraint(array, VMEM)


def in_smem(array):
    return pltpu.with_memory_space_constraint(array, SMEM)


def in_hbm(array):
    return pltpu.with_memory_space_constraint(array, pltpu.HBM)


vmem_spec = pl.BlockSpec(memory_space=VMEM)
smem_spec = pl.BlockSpec(memory_space=SMEM)
any_spec = pl.BlockSpec(memory_space=pl.ANY)


def params(mib):
    return pltpu.CompilerParams(vmem_limit_bytes=mib * MIB)


def cost(flops, moved):
    return pl.CostEstimate(flops=flops, bytes_accessed=moved, transcendentals=0)


def split(value):
    high = value.astype(bf16)
    return high, (value - high.astype(f32)).astype(bf16)


def store_split(ref, index, value):
    rows = value.shape[0]
    high, low = split(value)
    ref[index, 0:rows] = high
    ref[index, rows : 2 * rows] = low


def fold(product, rows):
    return (product[:rows, :128] + product[:rows, 128:]) + (product[rows:, :128] + product[rows:, 128:])


def lanes(block):
    return pl.ds(pl.multiple_of(block * 128, 128), 128)


def partner(value, apart):
    rows = value.shape[0]
    up = pltpu.roll(value, rows - apart, 0)
    down = pltpu.roll(value, apart, 0)
    place = lax.broadcasted_iota(jnp.int32, value.shape, 0)
    return jnp.where((place & apart) == 0, up, down)


def local_mean(value, members):
    total, apart = value, 1
    while apart < members:
        total = total + partner(total, apart)
        apart *= 2
    return total / members


def spread(pair, scenarios):
    count, width = pair.shape
    wide = jnp.broadcast_to(pair[:, None, :], (count, scenarios, width))
    return wide.reshape(count * scenarios, width)


def copies_of(pairs, sems):
    copies = [pltpu.make_async_copy(source, target, sems.at[n]) for n, (source, target) in enumerate(pairs)]
    for copy in copies:
        copy.start()
    return copies


def first_kernel(shared, per, small, send, start, *refs):
    sources, refs = refs[:small], refs[small:]
    sums, targets = refs[:shared], refs[shared : shared + small]
    send_out, head, sems = refs[shared + small :]
    cuts = [pl.ds(k * per, per) for k in range(shared)]
    pairs = [(start.at[cut], head.at[cut]) for cut in cuts] + list(zip(sources, targets))
    copies = copies_of(pairs, sems)
    for k in range(shared):
        copies[k].wait()
        sums[k][...] = jnp.sum(head[k * per : (k + 1) * per], axis=1)
    send_out[0] = send[0]
    for copy in copies[shared:]:
        copy.wait()


def add_kernel(count, *refs):
    for k in range(count):
        refs[-count + k][...] = refs[k][...] + refs[count + k][...]


def node_totals(sums, beside):
    shared = len(sums)
    totals = list(sums)
    done = sums[0]
    for turn in range(shared):
        active = [k for k in range(shared) if shared - k - 1 - turn >= 0]
        received = [swap(totals[k], "scen", shared - k - 1 - turn) for k in active]
        after = beside(turn, done)
        added = pl.pallas_call(
            functools.partial(add_kernel, len(active)),
            in_specs=[vmem_spec] * (2 * len(active)) + [any_spec] * len(after),
            out_specs=[vmem_spec] * len(active),
            out_shape=[VMEM(totals[k].shape, f32) for k in active],
            compiler_params=params(2),
            name=f"node_add_{turn}",
        )(*[in_vmem(totals[k]) for k in active], *[in_vmem(r) for r in received], *after)
        for k, value in zip(active, added):
            totals[k] = value
        done = added[0]
    return totals


def swap(block, axis, level):
    count = lax.axis_size(axis)
    return lax.ppermute(block, axis, [(i, i ^ (1 << level)) for i in range(count)])


def from_pair(value, axis):
    count = lax.axis_size(axis)
    return lax.ppermute(value, axis, [(i, i ^ 1) for i in range(count)])


def from_other(value, axis):
    count = lax.axis_size(axis)
    return lax.ppermute(value, axis, [(i, (i + 1 if i % 2 else i - 1) % count) for i in range(count)])


def lay_out(shared, per, scen_all, first, count, chunk, inputs, load, arrays, buffers, sems, between=None):
    weights, state, parts, constant = arrays
    values, start, mult, demand = buffers
    rows = state.shape[1]
    scenarios = start.shape[1]
    group = per * scenarios
    pairs = []
    for c in range(0, count, chunk):
        span = pl.ds(first + c, chunk)
        wide = pl.ds((first + c) * 128, chunk * 128)
        here = pl.ds(c * 128, chunk * 128)
        pairs += [
            (inputs[0].at[span], values.at[pl.ds(c, chunk)]),
            (inputs[1].at[:, :, wide], start.at[:, :, here]),
            (inputs[2].at[:, :, wide], mult.at[:, :, here]),
            (inputs[3].at[:, wide], demand.at[:, here]),
        ]
    copies = copies_of(pairs, sems)
    if between is not None:
        between()

    def one(b, carry):
        i = first + b
        for j in range(2):
            high, low = split(values[b, j] * -step_size)
            weights[i, j * 128 : (j + 1) * 128, 0:128] = high
            weights[i, j * 128 : (j + 1) * 128, 128:256] = low
        for k in range(rows // group):
            cut = slice(k * group, (k + 1) * group)
            span = slice(k * per, (k + 1) * per)
            x = start[span, :, lanes(b)].reshape(group, 128)
            m = mult[span, :, lanes(b)].reshape(group, 128)
            rest = m - spread(demand[span, lanes(b)], scenarios) * load[cut]
            if k >= shared:
                rest = rest - penalty * local_mean(x, max(scen_all >> k, 1))
            constant[i, cut] = -step_size * rest
            state[i, cut] = x
        store_split(parts, i, state[i])
        return carry

    for n, c in enumerate(range(0, count, chunk)):
        for copy in copies[4 * n : 4 * n + 4]:
            copy.wait()
        lax.fori_loop(c, c + chunk, one, 0, unroll=chunk)


def prepare_kernel(shared, per, scen_all, count, chunk, send, tie_source, node_ids, load_factor,
                   values, start, mult, demand, tie_weight,
                   weights, state, parts, constant, ties, load, boundary, *scratch):
    buffers, tie_buffer, block, sems = scratch[:4], scratch[4], scratch[5], scratch[6]
    scenarios = start.shape[1]
    extra = sems.shape[0] - 2
    copy_block = pltpu.make_async_copy(start.at[:, :, lanes(send[0])], block, sems.at[extra])
    copy_ties = pltpu.make_async_copy(tie_weight, tie_buffer, sems.at[extra + 1])
    copy_block.start()
    copy_ties.start()

    def between():
        for k in range(node_ids.shape[1]):
            for s in range(scenarios):
                row = jnp.full((1, 128), load_factor[node_ids[s, k]], f32)
                for t in range(per):
                    at = (k * per + t) * scenarios + s
                    load[at : at + 1] = row
        copy_block.wait()
        boundary[...] = block[...].reshape(boundary.shape)
        copy_ties.wait()
        mine = lax.axis_index("area")
        zero = jnp.zeros((128, 128), f32)
        for m in range(tie_weight.shape[0]):
            high, low = split(tie_buffer[m] * -step_size)
            from_partner = jnp.full((128, 128), tie_source[m] // send.shape[0], jnp.int32) == (mine ^ 1)
            for n, part in enumerate((high.astype(f32), low.astype(f32))):
                cut = slice(n * 128, (n + 1) * 128)
                ties[m, 0:128, cut] = jnp.where(from_partner, part, zero).astype(bf16)
                ties[m, 128:256, cut] = jnp.where(from_partner, zero, part).astype(bf16)

    lay_out(shared, per, scen_all, 0, count, chunk, (values, start, mult, demand), load,
            (weights, state, parts, constant), buffers, sems, between)


def prepare_more(shared, per, scen_all, first, count, chunk, values, start, mult, demand, load, after,
                 w_in, s_in, p_in, c_in, weights, state, parts, constant, *scratch):
    lay_out(shared, per, scen_all, first, count, chunk, (values, start, mult, demand), load,
            (weights, state, parts, constant), scratch[:4], scratch[4])


def step_kernel(cols, weights, state, parts, constant, new_state, new_parts):
    rows = state.shape[1]
    for i in range(state.shape[0]):
        other = cols[1, i]
        left = jnp.concatenate([parts[i], parts[other]], axis=1)
        product = jnp.dot(left, weights[i], preferred_element_type=f32)
        value = (keep * state[i] + constant[i]) + fold(product, rows)
        new_state[i] = value
        store_split(new_parts, i, value)


def add_ties(tie_row, low, high, ties, state, parts):
    rows = state.shape[1]
    both = jnp.concatenate([low[...], high[...]], axis=1)
    left = jnp.concatenate(split(both), axis=0)
    for m in range(ties.shape[0]):
        added = fold(jnp.dot(left, ties[m], preferred_element_type=f32), rows)
        row = tie_row[m]
        state[row] = state[row] + added
    for m in range(ties.shape[0]):
        row = tie_row[m]
        store_split(parts, row, state[row])


def tie_kernel(tie_row, send, low, high, ties, state_in, parts_in, state, parts, boundary):
    add_ties(tie_row, low, high, ties, state, parts)
    boundary[...] = state[send[0]]


def anchor_kernel(shared, scen_all, scenarios, tie_row, send, low, high, ties, *refs):
    totals = refs[:shared]
    state, parts, constant, boundary = refs[shared + 3 :]
    rows = state.shape[1]
    group = totals[0].shape[0] * scenarios
    span = min(-(-shared * group // 16) * 16, rows)

    def one(i, carry):
        for k in range(shared):
            cut = slice(k * group, (k + 1) * group)
            mean = spread(totals[k][:, lanes(i)], scenarios) / (scen_all >> k)
            mean = (step_size * penalty) * mean
            constant[i, cut] = constant[i, cut] + mean
            state[i, cut] = state[i, cut] + mean
        high_part, low_part = split(state[i, 0:span])
        parts[i, 0:span] = high_part
        parts[i, rows : rows + span] = low_part
        return carry

    lax.fori_loop(0, state.shape[0], one, 0, unroll=7)
    add_ties(tie_row, low, high, ties, state, parts)
    boundary[...] = state[send[0]]


def last_tie_kernel(shared, per, scenarios, tie_row, low, high, ties, state_in, parts_in, state, *refs):
    sums, parts = refs[:shared], refs[shared]
    add_ties(tie_row, low, high, ties, state, parts)
    group = per * scenarios

    def one(i, carry):
        for k in range(shared):
            piece = state[i, k * group : (k + 1) * group].reshape(per, scenarios, 128)
            sums[k][:, lanes(i)] = jnp.sum(piece, axis=1)
        return carry

    lax.fori_loop(0, state.shape[0], one, 0, unroll=7)


def write_blocks(pieces, blocks, one, buffer, out, sems, reads=None):
    width = blocks // pieces
    copies = []
    for piece in range(pieces):
        if reads is not None:
            reads[piece].wait()
        lax.fori_loop(piece * width, (piece + 1) * width, one, 0, unroll=largest_divisor(width, 7))
        cut = pl.ds(piece * width * 128, width * 128)
        copies.append(pltpu.make_async_copy(buffer.at[:, :, cut], out.at[:, :, cut], sems.at[piece]))
        copies[-1].start()
    for copy in copies:
        copy.wait()


def dispatch_kernel(pieces, state, mult, dispatch, mult_head, buffer, sems):
    head = pltpu.make_async_copy(mult.at[0 : mult_head.shape[0]], mult_head, sems.at[pieces])
    head.start()

    def one(i, carry):
        buffer[:, :, lanes(i)] = state[i].reshape(buffer.shape[0], buffer.shape[1], 128)
        return carry

    write_blocks(pieces, state.shape[0], one, buffer, dispatch, sems)
    head.wait()


def own_kernel(shared, per, scen_all, pieces, state, mult, after, new_mult, buffer, old_buffer, sems):
    scenarios = buffer.shape[1]
    blocks = state.shape[0]
    width = blocks // pieces
    cuts = [pl.ds(piece * width * 128, width * 128) for piece in range(pieces)]
    tail = mult.at[shared * per :]
    reads = [
        pltpu.make_async_copy(tail.at[:, :, cut], old_buffer.at[:, :, cut], sems.at[pieces + n])
        for n, cut in enumerate(cuts)
    ]
    for read in reads:
        read.start()
    group = per * scenarios

    def one(i, carry):
        for k in range(shared, state.shape[1] // group):
            value = state[i, k * group : (k + 1) * group]
            gap = penalty * (value - local_mean(value, max(scen_all >> k, 1)))
            cut = slice((k - shared) * per, (k - shared + 1) * per)
            buffer[cut, :, lanes(i)] = old_buffer[cut, :, lanes(i)] + gap.reshape(per, scenarios, 128)
        return carry

    write_blocks(pieces, blocks, one, buffer, new_mult.at[shared * per :], sems, reads)


def finish_kernel(shared, per, scen_all, pieces, state, mult, *refs):
    totals = refs[:shared]
    new_in, new_mult, buffer, sems = refs[shared:]
    scenarios = buffer.shape[1]
    group = per * scenarios

    def one(i, carry):
        for k in range(shared):
            value = state[i, k * group : (k + 1) * group]
            mean = spread(totals[k][:, lanes(i)], scenarios) / (scen_all >> k)
            gap = penalty * (value - mean)
            cut = slice(k * per, (k + 1) * per)
            buffer[cut, :, lanes(i)] = mult[cut, :, lanes(i)] + gap.reshape(per, scenarios, 128)
        return carry

    write_blocks(pieces, state.shape[0], one, buffer, new_mult.at[0 : shared * per], sems)


def largest_divisor(count, most):
    return max(d for d in range(1, most + 1) if count % d == 0)


def local(
    start_dispatch,
    multipliers,
    demand,
    load_factor,
    node_ids,
    block_values,
    block_cols,
    send_block,
    tie_source,
    tie_row,
    tie_weight,
):
    periods, scenarios, buses = start_dispatch.shape
    blocks = buses // 128
    rows = periods * scenarios
    sections = node_ids.shape[0]
    per = periods // sections
    devices = lax.axis_size("scen")
    scen_all = scenarios * devices
    shared = devices.bit_length() - 1
    tie_count = tie_row.shape[0]

    small = [block_cols.T, tie_row, tie_source, node_ids.T, load_factor]
    first = pl.pallas_call(
        functools.partial(first_kernel, shared, per, len(small)),
        in_specs=[smem_spec] + [any_spec] * (1 + len(small)),
        out_specs=[vmem_spec] * shared + [smem_spec] * (len(small) + 1),
        out_shape=[VMEM((per, buses), f32)] * shared + [SMEM(a.shape, a.dtype) for a in small + [send_block]],
        scratch_shapes=[
            VMEM((shared * per, scenarios, buses), f32),
            pltpu.SemaphoreType.DMA((shared + len(small),)),
        ],
        compiler_params=params(4),
        name="first_sums",
    )(send_block, in_hbm(start_dispatch), *[in_hbm(a) for a in small])
    sums = list(first[:shared])
    cols, row_of_tie, source_of_tie, labels, factors, send = first[shared:]
    inputs = [in_hbm(a) for a in (block_values, start_dispatch, multipliers, demand)]

    state_shape = VMEM((blocks, rows, 128), f32)
    parts_shape = VMEM((blocks, 2 * rows, 128), bf16)

    laid_shapes = [VMEM((blocks, 256, 256), bf16), state_shape, parts_shape, state_shape]
    chunk = largest_divisor(blocks, 7)
    parts_of = blocks // chunk
    ends = [0, 2 * parts_of // 5 * chunk, 7 * parts_of // 10 * chunk, blocks]
    laid = {}

    def buffers(count):
        return [
            VMEM((count, 2, 128, 128), f32),
            VMEM((periods, scenarios, count * 128), f32),
            VMEM((periods, scenarios, count * 128), f32),
            VMEM((periods, count * 128), f32),
        ]

    def prepare(turn, after):
        if turn >= len(ends) - 1:
            return []
        count = ends[turn + 1] - ends[turn]
        copies = 4 * (count // chunk)
        if turn == 0:
            made = pl.pallas_call(
                functools.partial(prepare_kernel, shared, per, scen_all, count, chunk),
                in_specs=[smem_spec] * 4 + [any_spec] * 5,
                out_specs=[vmem_spec] * 7,
                out_shape=laid_shapes
                + [VMEM((tie_count, 256, 256), bf16), VMEM((rows, 128), f32), VMEM((rows, 128), f32)],
                scratch_shapes=buffers(count)
                + [
                    VMEM((tie_count, 128, 128), f32),
                    VMEM((periods, scenarios, 128), f32),
                    pltpu.SemaphoreType.DMA((copies + 2,)),
                ],
                compiler_params=params(9),
                cost_estimate=cost(10**9, 10**6),
                name="prepare_0",
            )(in_smem(send), in_smem(source_of_tie), in_smem(labels), in_smem(factors), *inputs, in_hbm(tie_weight))
            laid["arrays"], laid["small"] = made[:4], made[4:]
            return [in_vmem(made[5])]
        laid["arrays"] = pl.pallas_call(
            functools.partial(prepare_more, shared, per, scen_all, ends[turn], count, chunk),
            in_specs=[any_spec] * 4 + [vmem_spec] * 6,
            out_specs=[vmem_spec] * 4,
            out_shape=laid_shapes,
            input_output_aliases={6: 0, 7: 1, 8: 2, 9: 3},
            scratch_shapes=buffers(count) + [pltpu.SemaphoreType.DMA((copies,))],
            compiler_params=params(9),
            cost_estimate=cost(10**9, 10**6),
            name=f"prepare_{turn}",
        )(*inputs, in_vmem(laid["small"][1]), in_vmem(after), *[in_vmem(a) for a in laid["arrays"]])
        return [in_vmem(laid["arrays"][1])] if turn < len(ends) - 2 else []

    totals = node_totals(sums, prepare)
    for turn in range(shared, len(ends) - 1):
        prepare(turn, totals[0])
    weights, state, parts, constant = laid["arrays"]
    ties, load, boundary = laid["small"]
    for iteration in range(STEPS):
        low = from_pair(boundary, "area")
        high = from_other(boundary, "area")
        state, parts = pl.pallas_call(
            step_kernel,
            in_specs=[smem_spec] + [vmem_spec] * 4,
            out_specs=[vmem_spec] * 2,
            out_shape=[state_shape, parts_shape],
            compiler_params=params(2),
            cost_estimate=cost(blocks * 2 * rows * 256 * 256 * 2, 12 * 10**6),
            name=f"step_{iteration}",
        )(in_smem(cols), in_vmem(weights), in_vmem(state), in_vmem(parts), in_vmem(constant))
        tie_args = [in_vmem(low), in_vmem(high), in_vmem(ties)]
        if iteration == 0:
            state, parts, constant, boundary = pl.pallas_call(
                functools.partial(anchor_kernel, shared, scen_all, scenarios),
                in_specs=[smem_spec] * 2 + [vmem_spec] * (6 + shared),
                out_specs=[vmem_spec] * 4,
                out_shape=[state_shape, parts_shape, state_shape, VMEM((rows, 128), f32)],
                input_output_aliases={5 + shared: 0, 6 + shared: 1, 7 + shared: 2},
                compiler_params=params(2),
                name="anchor",
            )(in_smem(row_of_tie), in_smem(send), *tie_args, *[in_vmem(t) for t in totals],
              in_vmem(state), in_vmem(parts), in_vmem(constant))
        elif iteration < STEPS - 1:
            state, parts, boundary = pl.pallas_call(
                tie_kernel,
                in_specs=[smem_spec] * 2 + [vmem_spec] * 5,
                out_specs=[vmem_spec] * 3,
                out_shape=[state_shape, parts_shape, VMEM((rows, 128), f32)],
                input_output_aliases={5: 0, 6: 1},
                compiler_params=params(2),
                name=f"ties_{iteration}",
            )(in_smem(row_of_tie), in_smem(send), *tie_args, in_vmem(state), in_vmem(parts))
        else:
            last = pl.pallas_call(
                functools.partial(last_tie_kernel, shared, per, scenarios),
                in_specs=[smem_spec] + [vmem_spec] * 5,
                out_specs=[vmem_spec] * (2 + shared),
                out_shape=[state_shape] + [VMEM((per, buses), f32)] * shared + [parts_shape],
                input_output_aliases={4: 0, 5: 1 + shared},
                compiler_params=params(2),
                name=f"ties_{iteration}",
            )(in_smem(row_of_tie), *tie_args, in_vmem(state), in_vmem(parts))
            state, sums = last[0], list(last[1 : 1 + shared])

    state = in_vmem(state)
    pieces = largest_divisor(blocks, 7)
    written = {}

    def write(turn, after):
        if turn == 0:
            written["dispatch"], written["head"] = pl.pallas_call(
                functools.partial(dispatch_kernel, pieces),
                in_specs=[vmem_spec, any_spec],
                out_specs=[any_spec, vmem_spec],
                out_shape=[
                    pltpu.HBM((periods, scenarios, buses), f32),
                    VMEM((shared * per, scenarios, buses), f32),
                ],
                scratch_shapes=[VMEM((periods, scenarios, buses), f32), pltpu.SemaphoreType.DMA((pieces + 1,))],
                compiler_params=params(6),
                cost_estimate=cost(10**9, 10**6),
                name="dispatch",
            )(state, in_hbm(multipliers))
            return [in_hbm(written["dispatch"])]
        if turn == 1:
            tail = VMEM((periods - shared * per, scenarios, buses), f32)
            written["mult"] = pl.pallas_call(
                functools.partial(own_kernel, shared, per, scen_all, pieces),
                in_specs=[vmem_spec, any_spec, vmem_spec],
                out_specs=any_spec,
                out_shape=pltpu.HBM((periods, scenarios, buses), f32),
                scratch_shapes=[tail, tail, pltpu.SemaphoreType.DMA((2 * pieces,))],
                compiler_params=params(8),
                cost_estimate=cost(10**9, 10**6),
                name="own_multipliers",
            )(state, in_hbm(multipliers), in_vmem(after))
            return [in_hbm(written["mult"])]
        return []

    totals = node_totals(sums, write)
    dispatch = written["dispatch"]
    new_mult = pl.pallas_call(
        functools.partial(finish_kernel, shared, per, scen_all, pieces),
        in_specs=[vmem_spec] * (2 + shared) + [any_spec],
        out_specs=any_spec,
        out_shape=pltpu.HBM((periods, scenarios, buses), f32),
        input_output_aliases={2 + shared: 0},
        scratch_shapes=[VMEM((shared * per, scenarios, buses), f32), pltpu.SemaphoreType.DMA((pieces,))],
        compiler_params=params(6),
        name="finish",
    )(state, in_vmem(written["head"]), *[in_vmem(t) for t in totals], in_hbm(written["mult"]))
    return dispatch, new_mult


def solution(mesh):
    in_specs = (
        P(None, "scen", "area"),
        P(None, "scen", "area"),
        P(None, "area"),
        P(),
        P(None, "scen"),
        P("area", None, None, None),
        P("area", None),
        P("area"),
        P("area"),
        P("area"),
        P("area", None, None),
    )
    out_specs = (P(None, "scen", "area"), P(None, "scen", "area"))
    return jax.shard_map(local, mesh=mesh, in_specs=in_specs, out_specs=out_specs, check_vma=False)
```

```python
import functools

import jax
import jax.numpy as jnp
from jax import lax
from jax.experimental import pallas as pl
from jax.experimental.pallas import tpu as pltpu
from jax.sharding import PartitionSpec as P

STEPS = 8
step_size = 0.25
penalty = 1.0
keep = 1.0 - step_size * penalty

f32 = jnp.float32
bf16 = jnp.bfloat16
VMEM = pltpu.VMEM
SMEM = pltpu.SMEM
MIB = 1 << 20


def in_vmem(array):
    return pltpu.with_memory_space_constraint(array, VMEM)


def in_smem(array):
    return pltpu.with_memory_space_constraint(array, SMEM)


def in_hbm(array):
    return pltpu.with_memory_space_constraint(array, pltpu.HBM)


vmem_spec = pl.BlockSpec(memory_space=VMEM)
smem_spec = pl.BlockSpec(memory_space=SMEM)
any_spec = pl.BlockSpec(memory_space=pl.ANY)


def params(mib):
    return pltpu.CompilerParams(vmem_limit_bytes=mib * MIB)


def cost(flops, moved):
    return pl.CostEstimate(flops=flops, bytes_accessed=moved, transcendentals=0)


def split(value):
    high = value.astype(bf16)
    return high, (value - high.astype(f32)).astype(bf16)


def store_split(ref, index, value):
    rows = value.shape[0]
    high, low = split(value)
    ref[index, 0:rows] = high
    ref[index, rows : 2 * rows] = low


def fold(product, rows):
    return (product[:rows, :128] + product[:rows, 128:]) + (product[rows:, :128] + product[rows:, 128:])


def lanes(block):
    return pl.ds(pl.multiple_of(block * 128, 128), 128)


def partner(value, apart):
    rows = value.shape[0]
    up = pltpu.roll(value, rows - apart, 0)
    down = pltpu.roll(value, apart, 0)
    place = lax.broadcasted_iota(jnp.int32, value.shape, 0)
    return jnp.where((place & apart) == 0, up, down)


def local_mean(value, members):
    total, apart = value, 1
    while apart < members:
        total = total + partner(total, apart)
        apart *= 2
    return total * (1.0 / members)


def spread(pair, scenarios):
    count, width = pair.shape
    wide = jnp.broadcast_to(pair[:, None, :], (count, scenarios, width))
    return wide.reshape(count * scenarios, width)


def copies_of(pairs, sems):
    copies = [pltpu.make_async_copy(source, target, sems.at[n]) for n, (source, target) in enumerate(pairs)]
    for copy in copies:
        copy.start()
    return copies


def first_kernel(shared, per, small, send, start, *refs):
    sources, refs = refs[:small], refs[small:]
    sums, targets = refs[:shared], refs[shared : shared + small]
    send_out, head, sems = refs[shared + small :]
    cuts = [pl.ds(k * per, per) for k in range(shared)]
    pairs = [(start.at[cut], head.at[cut]) for cut in cuts] + list(zip(sources, targets))
    copies = copies_of(pairs, sems)
    for k in range(shared):
        copies[k].wait()
        sums[k][...] = jnp.sum(head[k * per : (k + 1) * per], axis=1)
    send_out[0] = send[0]
    for copy in copies[shared:]:
        copy.wait()


def add_kernel(count, *refs):
    for k in range(count):
        refs[-count + k][...] = refs[k][...] + refs[count + k][...]


def node_totals(sums, beside):
    shared = len(sums)
    totals = list(sums)
    for turn in range(shared):
        active = [k for k in range(shared) if shared - k - 1 - turn >= 0]
        received = [swap(totals[k], "scen", shared - k - 1 - turn) for k in active]
        after = beside(turn, totals)
        added = pl.pallas_call(
            functools.partial(add_kernel, len(active)),
            in_specs=[vmem_spec] * (2 * len(active)) + [any_spec] * len(after),
            out_specs=[vmem_spec] * len(active),
            out_shape=[VMEM(totals[k].shape, f32) for k in active],
            compiler_params=params(2),
            name=f"node_add_{turn}",
        )(*[in_vmem(totals[k]) for k in active], *[in_vmem(r) for r in received], *after)
        for k, value in zip(active, added):
            totals[k] = value
    return totals


def swap(block, axis, level):
    count = lax.axis_size(axis)
    apart = 6 if level == 2 else 1 << level
    return lax.ppermute(block, axis, [(i, i ^ apart) for i in range(count)])


def from_pair(value, axis):
    count = lax.axis_size(axis)
    return lax.ppermute(value, axis, [(i, i ^ 1) for i in range(count)])


def from_other(value, axis):
    count = lax.axis_size(axis)
    return lax.ppermute(value, axis, [(i, (i + 1 if i % 2 else i - 1) % count) for i in range(count)])


def prepare_kernel(shared, per, scen_all, send, tie_source, node_ids, load_factor,
                   start, mult, demand, tie_weight, state, parts, constant, ties, load, boundary):
    rows = state.shape[1]
    scenarios = start.shape[1]
    group = per * scenarios
    for k in range(node_ids.shape[1]):
        for s in range(scenarios):
            row = jnp.full((1, 128), load_factor[node_ids[s, k]], f32)
            for t in range(per):
                at = (k * per + t) * scenarios + s
                load[at : at + 1] = row
    boundary[...] = start[:, :, lanes(send[0])].reshape(boundary.shape)
    mine = lax.axis_index("area")
    zero = jnp.zeros((128, 128), f32)
    for m in range(tie_weight.shape[0]):
        high, low = split(tie_weight[m] * -step_size)
        from_partner = jnp.full((128, 128), tie_source[m] // send.shape[0], jnp.int32) == (mine ^ 1)
        for n, part in enumerate((high.astype(f32), low.astype(f32))):
            cut = slice(n * 128, (n + 1) * 128)
            ties[m, 0:128, cut] = jnp.where(from_partner, zero, part).astype(bf16)
            ties[m, 128:256, cut] = jnp.where(from_partner, part, zero).astype(bf16)

    def one(i, carry):
        for k in range(rows // group):
            cut = slice(k * group, (k + 1) * group)
            span = slice(k * per, (k + 1) * per)
            x = start[span, :, lanes(i)].reshape(group, 128)
            m = mult[span, :, lanes(i)].reshape(group, 128)
            rest = m - spread(demand[span, lanes(i)], scenarios) * load[cut]
            if k >= shared:
                rest = rest - penalty * local_mean(x, max(scen_all >> k, 1))
            constant[i, cut] = -step_size * rest
            state[i, cut] = x
        store_split(parts, i, state[i])
        return carry

    lax.fori_loop(0, state.shape[0], one, 0, unroll=largest_divisor(state.shape[0], 7))


def advance(i, other, weight, state, parts, constant, new_state, new_parts):
    left = jnp.concatenate([parts[i], parts[other]], axis=1)
    product = jnp.dot(left, weight, preferred_element_type=f32)
    value = (keep * state[i] + constant[i]) + fold(product, state.shape[1])
    new_state[i] = value
    store_split(new_parts, i, value)
    return value


def first_step(first, count, cols, values, state, parts, constant, weights, new_state, new_parts):
    for i in range(first, first + count):
        for j in range(2):
            high, low = split(values[i, j] * -step_size)
            weights[i, j * 128 : (j + 1) * 128, 0:128] = high
            weights[i, j * 128 : (j + 1) * 128, 128:256] = low
        advance(i, cols[1, i], weights[i], state, parts, constant, new_state, new_parts)


def first_step_begin(first, count, cols, values, state, parts, constant, after, *refs):
    first_step(first, count, cols, values, state, parts, constant, *refs)


def first_step_end(first, count, cols, values, state, parts, constant, after, w_in, s_in, p_in, *refs):
    first_step(first, count, cols, values, state, parts, constant, *refs)


def step_kernel(cols, weights, state, parts, constant, spare_state, spare_parts, new_state, new_parts):
    for i in range(state.shape[0]):
        advance(i, cols[1, i], weights[i], state, parts, constant, new_state, new_parts)


def add_sums(shared, per, scenarios, i, value, sums):
    group = per * scenarios
    for k in range(shared):
        piece = value[k * group : (k + 1) * group].reshape(per, scenarios, 128)
        sums[k][:, lanes(i)] = jnp.sum(piece, axis=1)


def last_step_kernel(shared, per, scenarios, cols, weights, state, parts, constant, spare_state, spare_parts,
                     new_state, new_parts, *sums):
    for i in range(state.shape[0]):
        value = advance(i, cols[1, i], weights[i], state, parts, constant, new_state, new_parts)
        add_sums(shared, per, scenarios, i, value, sums)


def add_ties(tie_row, low, high, ties, state):
    rows = state.shape[1]
    both = jnp.concatenate([low[...], high[...]], axis=1)
    left = jnp.concatenate(split(both), axis=0)
    count = ties.shape[0]
    added = [fold(jnp.dot(left, ties[m], preferred_element_type=f32), rows) for m in range(count)]
    values = []
    for m in range(count):
        total = state[tie_row[m]]
        for n in range(count):
            same = jnp.where(tie_row[n] == tie_row[m], 1.0, 0.0)
            total = total + (added[n] if n == m else same * added[n])
        values.append(total)
    for m in range(count):
        state[tie_row[m]] = values[m]
    return values


def put_parts(tie_row, values, parts):
    for m, value in enumerate(values):
        store_split(parts, tie_row[m], value)


def tie_kernel(tie_row, send, low, high, ties, state_in, parts_in, state, parts, boundary):
    put_parts(tie_row, add_ties(tie_row, low, high, ties, state), parts)
    boundary[...] = state[send[0]]


def anchor_kernel(shared, scen_all, scenarios, tie_row, send, low, high, ties, *refs):
    totals = refs[:shared]
    state, parts, constant, boundary = refs[shared + 3 :]
    rows = state.shape[1]
    group = totals[0].shape[0] * scenarios
    span = min(-(-shared * group // 16) * 16, rows)

    def one(i, carry):
        for k in range(shared):
            cut = slice(k * group, (k + 1) * group)
            mean = spread(totals[k][:, lanes(i)], scenarios) * (1.0 / (scen_all >> k))
            mean = (step_size * penalty) * mean
            constant[i, cut] = constant[i, cut] + mean
            state[i, cut] = state[i, cut] + mean
        high_part, low_part = split(state[i, 0:span])
        parts[i, 0:span] = high_part
        parts[i, rows : rows + span] = low_part
        return carry

    lax.fori_loop(0, state.shape[0], one, 0, unroll=largest_divisor(state.shape[0], 14))
    put_parts(tie_row, add_ties(tie_row, low, high, ties, state), parts)
    boundary[...] = state[send[0]]


def last_tie_kernel(shared, per, scenarios, tie_row, low, high, ties, *refs):
    state, sums = refs[shared + 1], refs[shared + 2 :]
    values = add_ties(tie_row, low, high, ties, state)
    for m, value in enumerate(values):
        add_sums(shared, per, scenarios, tie_row[m], value, sums)


def write_blocks(pieces, blocks, one, buffer, out, sems):
    width = blocks // pieces
    copies = []
    for piece in range(pieces):
        lax.fori_loop(piece * width, (piece + 1) * width, one, 0, unroll=largest_divisor(width, 7))
        cut = pl.ds(piece * width * 128, width * 128)
        copies.append(pltpu.make_async_copy(buffer.at[:, :, cut], out.at[:, :, cut], sems.at[piece]))
        copies[-1].start()
    for copy in copies:
        copy.wait()


def dispatch_kernel(pieces, state, dispatch, buffer, sems):
    def one(i, carry):
        buffer[:, :, lanes(i)] = state[i].reshape(buffer.shape[0], buffer.shape[1], 128)
        return carry

    write_blocks(pieces, state.shape[0], one, buffer, dispatch, sems)


def multiplier_kernel(sections, scen_all, pieces, state, mult, *refs):
    new_mult, buffer, sems = refs[-3:]
    totals = dict(zip(sections, refs[: -3]))
    per, scenarios = buffer.shape[0] // len(sections), buffer.shape[1]
    group = per * scenarios

    def one(i, carry):
        for n, k in enumerate(sections):
            value = state[i, k * group : (k + 1) * group]
            if scen_all >> k > scenarios:
                mean = spread(totals[k][:, lanes(i)], scenarios) * (1.0 / (scen_all >> k))
            else:
                mean = local_mean(value, max(scen_all >> k, 1))
            gap = penalty * (value - mean)
            old = mult[k * per : (k + 1) * per, :, lanes(i)]
            buffer[n * per : (n + 1) * per, :, lanes(i)] = old + gap.reshape(per, scenarios, 128)
        return carry

    rows = pl.ds(sections[0] * per, len(sections) * per)
    write_blocks(pieces, state.shape[0], one, buffer, new_mult.at[rows], sems)


def largest_divisor(count, most):
    return max(d for d in range(1, most + 1) if count % d == 0)


def local(
    start_dispatch,
    multipliers,
    demand,
    load_factor,
    node_ids,
    block_values,
    block_cols,
    send_block,
    tie_source,
    tie_row,
    tie_weight,
):
    periods, scenarios, buses = start_dispatch.shape
    blocks = buses // 128
    rows = periods * scenarios
    sections = node_ids.shape[0]
    per = periods // sections
    devices = lax.axis_size("scen")
    scen_all = scenarios * devices
    shared = devices.bit_length() - 1
    tie_count = tie_row.shape[0]

    small = [block_cols.T, tie_row, tie_source, node_ids.T, load_factor]
    first = pl.pallas_call(
        functools.partial(first_kernel, shared, per, len(small)),
        in_specs=[smem_spec] + [any_spec] * (1 + len(small)),
        out_specs=[vmem_spec] * shared + [smem_spec] * (len(small) + 1),
        out_shape=[VMEM((per, buses), f32)] * shared + [SMEM(a.shape, a.dtype) for a in small + [send_block]],
        scratch_shapes=[
            VMEM((shared * per, scenarios, buses), f32),
            pltpu.SemaphoreType.DMA((shared + len(small),)),
        ],
        compiler_params=params(4),
        cost_estimate=cost(2 * 10**10, 10**6),
        name="first_sums",
    )(send_block, in_hbm(start_dispatch), *[in_hbm(a) for a in small])
    sums = list(first[:shared])
    cols, row_of_tie, source_of_tie, labels, factors, send = first[shared:]

    state_shape = VMEM((blocks, rows, 128), f32)
    parts_shape = VMEM((blocks, 2 * rows, 128), bf16)

    weights_shape = VMEM((blocks, 256, 256), bf16)
    half = blocks // 2
    laid = {}

    def prepare(turn, totals):
        after = totals[0]
        if turn == 0:
            laid["start"] = pl.pallas_call(
                functools.partial(prepare_kernel, shared, per, scen_all),
                in_specs=[smem_spec] * 4 + [vmem_spec] * 4,
                out_specs=[vmem_spec] * 6,
                out_shape=[state_shape, parts_shape, state_shape]
                + [VMEM((tie_count, 256, 256), bf16), VMEM((rows, 128), f32), VMEM((rows, 128), f32)],
                compiler_params=params(2),
                cost_estimate=cost(10**9, 10**6),
                name="prepare",
            )(in_smem(send), in_smem(source_of_tie), in_smem(labels), in_smem(factors),
              *[in_vmem(a) for a in (start_dispatch, multipliers, demand, tie_weight)])
            return [in_vmem(laid["start"][5])]
        if turn > 2:
            return []
        first, count = (0, half) if turn == 1 else (half, blocks - half)
        held = [in_vmem(a) for a in laid["start"][:3]]
        made = [] if turn == 1 else [in_vmem(a) for a in laid["made"]]
        laid["made"] = pl.pallas_call(
            functools.partial(first_step_begin if turn == 1 else first_step_end, first, count),
            in_specs=[smem_spec] + [vmem_spec] * (5 + len(made)),
            out_specs=[vmem_spec] * 3,
            out_shape=[weights_shape, state_shape, parts_shape],
            input_output_aliases={} if turn == 1 else {6: 0, 7: 1, 8: 2},
            compiler_params=params(2),
            cost_estimate=cost(10**9, 10**6),
            name=f"step_0_{turn}",
        )(in_smem(cols), in_vmem(block_values), *held, in_vmem(after), *made)
        return [in_vmem(laid["made"][1])] if turn == 1 else []

    totals = node_totals(sums, prepare)
    for turn in range(shared, 3):
        prepare(turn, totals)
    spare_state, spare_parts, constant, ties, load, boundary = laid["start"]
    weights, state, parts = laid["made"]
    for iteration in range(STEPS):
        low = from_other(boundary, "area")
        high = from_pair(boundary, "area")
        tie_args = [in_vmem(low), in_vmem(high), in_vmem(ties)]
        if iteration == 0:
            state, parts, constant, boundary = pl.pallas_call(
                functools.partial(anchor_kernel, shared, scen_all, scenarios),
                in_specs=[smem_spec] * 2 + [vmem_spec] * (6 + shared),
                out_specs=[vmem_spec] * 4,
                out_shape=[state_shape, parts_shape, state_shape, VMEM((rows, 128), f32)],
                input_output_aliases={5 + shared: 0, 6 + shared: 1, 7 + shared: 2},
                compiler_params=params(2),
                name="anchor",
            )(in_smem(row_of_tie), in_smem(send), *tie_args, *[in_vmem(t) for t in totals],
              in_vmem(state), in_vmem(parts), in_vmem(constant))
            continue
        last = iteration == STEPS - 1
        used = (state, parts)
        made = pl.pallas_call(
            functools.partial(last_step_kernel, shared, per, scenarios) if last else step_kernel,
            in_specs=[smem_spec] + [vmem_spec] * 6,
            out_specs=[vmem_spec] * (2 + shared * last),
            out_shape=[state_shape, parts_shape] + [VMEM((per, buses), f32)] * (shared * last),
            input_output_aliases={5: 0, 6: 1},
            compiler_params=params(2),
            cost_estimate=cost(blocks * 2 * rows * 256 * 256 * 2, 12 * 10**6),
            name=f"step_{iteration}",
        )(in_smem(cols), *[in_vmem(a) for a in (weights, state, parts, constant, spare_state, spare_parts)])
        state, parts = made[:2]
        spare_state, spare_parts = used
        if last:
            made = pl.pallas_call(
                functools.partial(last_tie_kernel, shared, per, scenarios),
                in_specs=[smem_spec] + [vmem_spec] * (4 + shared),
                out_specs=[vmem_spec] * (1 + shared),
                out_shape=[state_shape] + [VMEM((per, buses), f32)] * shared,
                input_output_aliases={4 + k: k for k in range(1 + shared)},
                compiler_params=params(2),
                name=f"ties_{iteration}",
            )(in_smem(row_of_tie), *tie_args, in_vmem(state), *[in_vmem(a) for a in made[2:]])
            state, sums = made[0], list(made[1:])
        else:
            state, parts, boundary = pl.pallas_call(
                tie_kernel,
                in_specs=[smem_spec] * 2 + [vmem_spec] * 5,
                out_specs=[vmem_spec] * 3,
                out_shape=[state_shape, parts_shape, VMEM((rows, 128), f32)],
                input_output_aliases={5: 0, 6: 1},
                compiler_params=params(2),
                name=f"ties_{iteration}",
            )(in_smem(row_of_tie), in_smem(send), *tie_args, in_vmem(state), in_vmem(parts))

    state = in_vmem(state)
    pieces = largest_divisor(blocks, 7)
    written = {}

    def multiply(chosen, totals, after):
        old = [in_hbm(written["mult"])] if "mult" in written else []
        extra = [in_vmem(t) for t in totals] + ([in_vmem(after)] if after is not None else [])
        written["mult"] = pl.pallas_call(
            functools.partial(multiplier_kernel, chosen, scen_all, pieces),
            in_specs=[vmem_spec] * (2 + len(extra)) + [any_spec] * len(old),
            out_specs=any_spec,
            out_shape=pltpu.HBM((periods, scenarios, buses), f32),
            input_output_aliases={2 + len(extra): 0} if old else {},
            scratch_shapes=[
                VMEM((len(chosen) * per, scenarios, buses), f32),
                pltpu.SemaphoreType.DMA((pieces,)),
            ],
            compiler_params=params(5),
            cost_estimate=cost(10**9, 10**6),
            name=f"multipliers_{chosen[0]}",
        )(state, in_vmem(multipliers), *extra, *old)
        return [in_hbm(written["mult"])]

    def write(turn, totals):
        if turn == 0:
            written["dispatch"] = pl.pallas_call(
                functools.partial(dispatch_kernel, pieces),
                in_specs=[vmem_spec],
                out_specs=any_spec,
                out_shape=pltpu.HBM((periods, scenarios, buses), f32),
                scratch_shapes=[VMEM((periods, scenarios, buses), f32), pltpu.SemaphoreType.DMA((pieces,))],
                compiler_params=params(5),
                cost_estimate=cost(10**9, 10**6),
                name="dispatch",
            )(state)
            return [in_hbm(written["dispatch"])]
        done = shared - turn
        chosen = list(range(done, sections if turn == 1 else done + 1))
        return multiply(chosen, [totals[done]], None)

    totals = node_totals(sums, write)
    dispatch = written["dispatch"]
    new_mult = multiply([0], [totals[0]], None)[0]
    return dispatch, new_mult


def solution(mesh):
    in_specs = (
        P(None, "scen", "area"),
        P(None, "scen", "area"),
        P(None, "area"),
        P(),
        P(None, "scen"),
        P("area", None, None, None),
        P("area", None),
        P("area"),
        P("area"),
        P("area"),
        P("area", None, None),
    )
    out_specs = (P(None, "scen", "area"), P(None, "scen", "area"))
    return jax.shard_map(local, mesh=mesh, in_specs=in_specs, out_specs=out_specs, check_vma=False)
```

```python
import functools

import jax
import jax.numpy as jnp
from jax import lax
from jax.experimental import pallas as pl
from jax.experimental.pallas import tpu as pltpu
from jax.sharding import PartitionSpec as P

STEPS = 8
step_size = 0.25
penalty = 1.0
keep = 1.0 - step_size * penalty

f32 = jnp.float32
bf16 = jnp.bfloat16
VMEM = pltpu.VMEM
SMEM = pltpu.SMEM
MIB = 1 << 20


def in_vmem(array):
    return pltpu.with_memory_space_constraint(array, VMEM)


def in_smem(array):
    return pltpu.with_memory_space_constraint(array, SMEM)


def in_hbm(array):
    return pltpu.with_memory_space_constraint(array, pltpu.HBM)


vmem_spec = pl.BlockSpec(memory_space=VMEM)
smem_spec = pl.BlockSpec(memory_space=SMEM)
any_spec = pl.BlockSpec(memory_space=pl.ANY)


def params(mib):
    return pltpu.CompilerParams(vmem_limit_bytes=mib * MIB)


def cost(flops, moved):
    return pl.CostEstimate(flops=flops, bytes_accessed=moved, transcendentals=0)


def split(value):
    high = value.astype(bf16)
    return high, (value - high.astype(f32)).astype(bf16)


def store_split(ref, index, value):
    rows = value.shape[0]
    high, low = split(value)
    ref[index, 0:rows] = high
    ref[index, rows : 2 * rows] = low


def fold(product, rows):
    return (product[:rows, :128] + product[:rows, 128:]) + (product[rows:, :128] + product[rows:, 128:])


def lanes(block):
    return pl.ds(pl.multiple_of(block * 128, 128), 128)


def partner(value, apart):
    rows = value.shape[0]
    up = pltpu.roll(value, rows - apart, 0)
    down = pltpu.roll(value, apart, 0)
    place = lax.broadcasted_iota(jnp.int32, value.shape, 0)
    return jnp.where((place & apart) == 0, up, down)


def local_mean(value, members):
    total, apart = value, 1
    while apart < members:
        total = total + partner(total, apart)
        apart *= 2
    return total * (1.0 / members)


def spread(ref, first, count, scenarios, block):
    shape = (count * scenarios, 128)
    place = lax.broadcasted_iota(jnp.int32, shape, 0)
    wide = jnp.broadcast_to(ref[first : first + 1, lanes(block)], shape)
    for t in range(1, count):
        row = jnp.broadcast_to(ref[first + t : first + t + 1, lanes(block)], shape)
        wide = jnp.where(place < t * scenarios, wide, row)
    return wide


def copies_of(pairs, sems):
    copies = [pltpu.make_async_copy(source, target, sems.at[n]) for n, (source, target) in enumerate(pairs)]
    for copy in copies:
        copy.start()
    return copies


def first_kernel(shared, per, small, send, start, *refs):
    sources, refs = refs[:small], refs[small:]
    sums, targets = refs[:shared], refs[shared : shared + small]
    send_out, head, sems = refs[shared + small :]
    cuts = [pl.ds(k * per, per) for k in range(shared)]
    pairs = [(start.at[cut], head.at[cut]) for cut in cuts] + list(zip(sources, targets))
    copies = copies_of(pairs, sems)
    for k in range(shared):
        copies[k].wait()
        sums[k][...] = jnp.sum(head[k * per : (k + 1) * per], axis=1)
    send_out[0] = send[0]
    for copy in copies[shared:]:
        copy.wait()


def add_kernel(counts, *refs):
    inputs, outputs = iter(refs), refs[-len(counts) :]
    for count, output in zip(counts, outputs):
        total = next(inputs)[...]
        for _ in range(count):
            total = total + next(inputs)[...]
        output[...] = total


def turns_of(levels, wide):
    if not wide:
        return [[1 << level] for level in reversed(range(levels))]
    if levels < 3:
        return [[1 << level] for level in range(levels)]
    low = 1 << (levels - 2)
    return [[low, 2 * low, 3 * low]] + turns_of(levels - 2, wide)


def swap(block, axis, apart):
    count = lax.axis_size(axis)
    return lax.ppermute(block, axis, [(i, i ^ apart) for i in range(count)])


def node_totals(sums, wide, beside):
    shared = len(sums)
    totals = list(sums)
    plans = [turns_of(shared - k, wide) for k in range(shared)]
    for turn in range(max(len(plan) for plan in plans)):
        active = [k for k in range(shared) if turn < len(plans[k])]
        operands = []
        for k in active:
            operands += [totals[k]] + [swap(totals[k], "scen", apart) for apart in plans[k][turn]]
        after = beside(turn, totals, [k for k in range(shared) if len(plans[k]) == turn])
        counts = [len(plans[k][turn]) for k in active]
        added = pl.pallas_call(
            functools.partial(add_kernel, counts),
            in_specs=[vmem_spec] * len(operands) + [any_spec] * len(after),
            out_specs=[vmem_spec] * len(active),
            out_shape=[VMEM(totals[k].shape, f32) for k in active],
            compiler_params=params(2),
            name=f"node_add_{turn}",
        )(*[in_vmem(a) for a in operands], *after)
        for k, value in zip(active, added):
            totals[k] = value
    return totals


def from_pair(value, axis):
    count = lax.axis_size(axis)
    return lax.ppermute(value, axis, [(i, i ^ 1) for i in range(count)])


def from_other(value, axis):
    count = lax.axis_size(axis)
    return lax.ppermute(value, axis, [(i, (i + 1 if i % 2 else i - 1) % count) for i in range(count)])


def prepare_kernel(shared, per, scen_all, send, tie_source, node_ids, load_factor,
                   start, mult, demand, tie_weight, state, parts, constant, ties, load, boundary):
    rows = state.shape[1]
    scenarios = start.shape[1]
    group = per * scenarios
    for k in range(node_ids.shape[1]):
        for s in range(scenarios):
            row = jnp.full((1, 128), load_factor[node_ids[s, k]], f32)
            for t in range(per):
                at = (k * per + t) * scenarios + s
                load[at : at + 1] = row
    boundary[...] = start[:, :, lanes(send[0])].reshape(boundary.shape)
    mine = lax.axis_index("area")
    zero = jnp.zeros((128, 128), f32)
    for m in range(tie_weight.shape[0]):
        high, low = split(tie_weight[m] * -step_size)
        from_partner = jnp.full((128, 128), tie_source[m] // send.shape[0], jnp.int32) == (mine ^ 1)
        for n, part in enumerate((high.astype(f32), low.astype(f32))):
            cut = slice(n * 128, (n + 1) * 128)
            ties[m, 0:128, cut] = jnp.where(from_partner, zero, part).astype(bf16)
            ties[m, 128:256, cut] = jnp.where(from_partner, part, zero).astype(bf16)

    def one(i, carry):
        for k in range(rows // group):
            cut = slice(k * group, (k + 1) * group)
            span = slice(k * per, (k + 1) * per)
            x = start[span, :, lanes(i)].reshape(group, 128)
            m = mult[span, :, lanes(i)].reshape(group, 128)
            rest = m - spread(demand, k * per, per, scenarios, i) * load[cut]
            if k >= shared:
                rest = rest - penalty * local_mean(x, max(scen_all >> k, 1))
            constant[i, cut] = -step_size * rest
            state[i, cut] = x
        store_split(parts, i, state[i])
        return carry

    lax.fori_loop(0, state.shape[0], one, 0, unroll=largest_divisor(state.shape[0], 7))


def advance(i, other, weight, state, parts, constant, new_state, new_parts):
    left = jnp.concatenate([parts[i], parts[other]], axis=1)
    product = jnp.dot(left, weight, preferred_element_type=f32)
    value = (keep * state[i] + constant[i]) + fold(product, state.shape[1])
    new_state[i] = value
    store_split(new_parts, i, value)
    return value


def first_step(first, count, cols, values, state, parts, constant, weights, new_state, new_parts):
    for i in range(first, first + count):
        for j in range(2):
            high, low = split(values[i, j] * -step_size)
            weights[i, j * 128 : (j + 1) * 128, 0:128] = high
            weights[i, j * 128 : (j + 1) * 128, 128:256] = low
        advance(i, cols[1, i], weights[i], state, parts, constant, new_state, new_parts)


def first_step_begin(first, count, cols, values, state, parts, constant, after, *refs):
    first_step(first, count, cols, values, state, parts, constant, *refs)


def first_step_end(first, count, cols, values, state, parts, constant, after, w_in, s_in, p_in, *refs):
    first_step(first, count, cols, values, state, parts, constant, *refs)


def step_kernel(cols, weights, state, parts, constant, spare_state, spare_parts, new_state, new_parts):
    for i in range(state.shape[0]):
        advance(i, cols[1, i], weights[i], state, parts, constant, new_state, new_parts)


def add_sums(shared, per, scenarios, i, value, sums):
    group = per * scenarios
    for k in range(shared):
        piece = value[k * group : (k + 1) * group].reshape(per, scenarios, 128)
        sums[k][:, lanes(i)] = jnp.sum(piece, axis=1)


def last_step_kernel(shared, per, scenarios, cols, weights, state, parts, constant, spare_state, spare_parts,
                     new_state, new_parts, *sums):
    for i in range(state.shape[0]):
        value = advance(i, cols[1, i], weights[i], state, parts, constant, new_state, new_parts)
        add_sums(shared, per, scenarios, i, value, sums)


def add_ties(tie_row, low, high, ties, state):
    rows = state.shape[1]
    both = jnp.concatenate([low[...], high[...]], axis=1)
    left = jnp.concatenate(split(both), axis=0)
    count = ties.shape[0]
    added = [fold(jnp.dot(left, ties[m], preferred_element_type=f32), rows) for m in range(count)]
    values = []
    for m in range(count):
        total = state[tie_row[m]]
        for n in range(count):
            same = jnp.where(tie_row[n] == tie_row[m], 1.0, 0.0)
            total = total + (added[n] if n == m else same * added[n])
        values.append(total)
    for m in range(count):
        state[tie_row[m]] = values[m]
    return values


def put_parts(tie_row, values, parts):
    for m, value in enumerate(values):
        store_split(parts, tie_row[m], value)


def tie_kernel(tie_row, send, low, high, ties, state_in, parts_in, state, parts, boundary):
    put_parts(tie_row, add_ties(tie_row, low, high, ties, state), parts)
    boundary[...] = state[send[0]]


def anchor_kernel(shared, scen_all, scenarios, tie_row, send, low, high, ties, *refs):
    totals = refs[:shared]
    state, parts, constant, boundary = refs[shared + 3 :]
    rows = state.shape[1]
    group = totals[0].shape[0] * scenarios
    span = min(-(-shared * group // 16) * 16, rows)

    def one(i, carry):
        for k in range(shared):
            cut = slice(k * group, (k + 1) * group)
            mean = spread(totals[k], 0, group // scenarios, scenarios, i) * (1.0 / (scen_all >> k))
            mean = (step_size * penalty) * mean
            constant[i, cut] = constant[i, cut] + mean
            state[i, cut] = state[i, cut] + mean
        high_part, low_part = split(state[i, 0:span])
        parts[i, 0:span] = high_part
        parts[i, rows : rows + span] = low_part
        return carry

    lax.fori_loop(0, state.shape[0], one, 0, unroll=largest_divisor(state.shape[0], 14))
    put_parts(tie_row, add_ties(tie_row, low, high, ties, state), parts)
    boundary[...] = state[send[0]]


def last_tie_kernel(shared, per, scenarios, tie_row, low, high, ties, *refs):
    state, sums = refs[shared + 1], refs[shared + 2 :]
    values = add_ties(tie_row, low, high, ties, state)
    for m, value in enumerate(values):
        add_sums(shared, per, scenarios, tie_row[m], value, sums)


def write_blocks(pieces, blocks, one, targets, sems):
    width = blocks // pieces
    copies = []
    for piece in range(pieces):
        lax.fori_loop(piece * width, (piece + 1) * width, one, 0, unroll=largest_divisor(width, 7))
        cut = pl.ds(piece * width * 128, width * 128)
        for buffer, out in targets:
            copies.append(pltpu.make_async_copy(buffer.at[:, :, cut], out.at[:, :, cut], sems.at[len(copies)]))
            copies[-1].start()
    for copy in copies:
        copy.wait()


def put_multipliers(chosen, scen_all, state, mult, totals, buffer, i):
    per, scenarios = buffer.shape[0] // len(chosen), buffer.shape[1]
    group = per * scenarios
    for n, k in enumerate(chosen):
        value = state[i, k * group : (k + 1) * group]
        if scen_all >> k > scenarios:
            mean = spread(totals[k], 0, per, scenarios, i) * (1.0 / (scen_all >> k))
        else:
            mean = local_mean(value, max(scen_all >> k, 1))
        gap = penalty * (value - mean)
        old = mult[k * per : (k + 1) * per, :, lanes(i)]
        buffer[n * per : (n + 1) * per, :, lanes(i)] = old + gap.reshape(per, scenarios, 128)


def output_kernel(chosen, scen_all, pieces, state, mult, dispatch, new_mult, whole, buffer, sems):
    periods, scenarios = whole.shape[:2]
    per = buffer.shape[0] // len(chosen)

    def one(i, carry):
        whole[:, :, lanes(i)] = state[i].reshape(periods, scenarios, 128)
        put_multipliers(chosen, scen_all, state, mult, {}, buffer, i)
        return carry

    rows = pl.ds(chosen[0] * per, len(chosen) * per)
    write_blocks(pieces, state.shape[0], one, [(whole, dispatch), (buffer, new_mult.at[rows])], sems)


def multiplier_kernel(chosen, scen_all, pieces, state, mult, *refs):
    new_mult, buffer, sems = refs[-3:]
    totals = dict(zip(chosen, refs[:-3]))
    per = buffer.shape[0] // len(chosen)

    def one(i, carry):
        put_multipliers(chosen, scen_all, state, mult, totals, buffer, i)
        return carry

    rows = pl.ds(chosen[0] * per, len(chosen) * per)
    write_blocks(pieces, state.shape[0], one, [(buffer, new_mult.at[rows])], sems)


def largest_divisor(count, most):
    return max(d for d in range(1, most + 1) if count % d == 0)


def local(
    start_dispatch,
    multipliers,
    demand,
    load_factor,
    node_ids,
    block_values,
    block_cols,
    send_block,
    tie_source,
    tie_row,
    tie_weight,
):
    periods, scenarios, buses = start_dispatch.shape
    blocks = buses // 128
    rows = periods * scenarios
    sections = node_ids.shape[0]
    per = periods // sections
    devices = lax.axis_size("scen")
    scen_all = scenarios * devices
    shared = devices.bit_length() - 1
    tie_count = tie_row.shape[0]

    small = [block_cols.T, tie_row, tie_source, node_ids.T, load_factor]
    first = pl.pallas_call(
        functools.partial(first_kernel, shared, per, len(small)),
        in_specs=[smem_spec] + [any_spec] * (1 + len(small)),
        out_specs=[vmem_spec] * shared + [smem_spec] * (len(small) + 1),
        out_shape=[VMEM((per, buses), f32)] * shared + [SMEM(a.shape, a.dtype) for a in small + [send_block]],
        scratch_shapes=[
            VMEM((shared * per, scenarios, buses), f32),
            pltpu.SemaphoreType.DMA((shared + len(small),)),
        ],
        compiler_params=params(4),
        cost_estimate=cost(2 * 10**10, 10**6),
        name="first_sums",
    )(send_block, in_hbm(start_dispatch), *[in_hbm(a) for a in small])
    sums = list(first[:shared])
    cols, row_of_tie, source_of_tie, labels, factors, send = first[shared:]

    state_shape = VMEM((blocks, rows, 128), f32)
    parts_shape = VMEM((blocks, 2 * rows, 128), bf16)

    weights_shape = VMEM((blocks, 256, 256), bf16)
    half = 2 * blocks // 7
    laid = {}

    def prepare(turn, totals, ready):
        after = totals[0]
        if turn == 0:
            laid["start"] = pl.pallas_call(
                functools.partial(prepare_kernel, shared, per, scen_all),
                in_specs=[smem_spec] * 4 + [vmem_spec] * 4,
                out_specs=[vmem_spec] * 6,
                out_shape=[state_shape, parts_shape, state_shape]
                + [VMEM((tie_count, 256, 256), bf16), VMEM((rows, 128), f32), VMEM((rows, 128), f32)],
                compiler_params=params(2),
                cost_estimate=cost(10**9, 10**6),
                name="prepare",
            )(in_smem(send), in_smem(source_of_tie), in_smem(labels), in_smem(factors),
              *[in_vmem(a) for a in (start_dispatch, multipliers, demand, tie_weight)])
        if turn > 1:
            return []
        first, count = (0, half) if turn == 0 else (half, blocks - half)
        held = [in_vmem(a) for a in laid["start"][:3]]
        made = [] if turn == 0 else [in_vmem(a) for a in laid["made"]]
        laid["made"] = pl.pallas_call(
            functools.partial(first_step_begin if turn == 0 else first_step_end, first, count),
            in_specs=[smem_spec] + [vmem_spec] * (5 + len(made)),
            out_specs=[vmem_spec] * 3,
            out_shape=[weights_shape, state_shape, parts_shape],
            input_output_aliases={} if turn == 0 else {6: 0, 7: 1, 8: 2},
            compiler_params=params(2),
            cost_estimate=cost(10**9, 10**6),
            name=f"step_0_{turn}",
        )(in_smem(cols), in_vmem(block_values), *held, in_vmem(after), *made)
        return [in_vmem(laid["made"][1])] if turn == 0 else []

    totals = node_totals(sums, True, prepare)
    if len(turns_of(shared, True)) < 2:
        prepare(1, totals, [])
    spare_state, spare_parts, constant, ties, load, boundary = laid["start"]
    weights, state, parts = laid["made"]
    for iteration in range(STEPS):
        low = from_other(boundary, "area")
        high = from_pair(boundary, "area")
        tie_args = [in_vmem(low), in_vmem(high), in_vmem(ties)]
        if iteration == 0:
            state, parts, constant, boundary = pl.pallas_call(
                functools.partial(anchor_kernel, shared, scen_all, scenarios),
                in_specs=[smem_spec] * 2 + [vmem_spec] * (6 + shared),
                out_specs=[vmem_spec] * 4,
                out_shape=[state_shape, parts_shape, state_shape, VMEM((rows, 128), f32)],
                input_output_aliases={5 + shared: 0, 6 + shared: 1, 7 + shared: 2},
                compiler_params=params(2),
                name="anchor",
            )(in_smem(row_of_tie), in_smem(send), *tie_args, *[in_vmem(t) for t in totals],
              in_vmem(state), in_vmem(parts), in_vmem(constant))
            continue
        last = iteration == STEPS - 1
        used = (state, parts)
        made = pl.pallas_call(
            functools.partial(last_step_kernel, shared, per, scenarios) if last else step_kernel,
            in_specs=[smem_spec] + [vmem_spec] * 6,
            out_specs=[vmem_spec] * (2 + shared * last),
            out_shape=[state_shape, parts_shape] + [VMEM((per, buses), f32)] * (shared * last),
            input_output_aliases={5: 0, 6: 1},
            compiler_params=params(2),
            cost_estimate=cost(blocks * 2 * rows * 256 * 256 * 2, 12 * 10**6),
            name=f"step_{iteration}",
        )(in_smem(cols), *[in_vmem(a) for a in (weights, state, parts, constant, spare_state, spare_parts)])
        state, parts = made[:2]
        spare_state, spare_parts = used
        if last:
            made = pl.pallas_call(
                functools.partial(last_tie_kernel, shared, per, scenarios),
                in_specs=[smem_spec] + [vmem_spec] * (4 + shared),
                out_specs=[vmem_spec] * (1 + shared),
                out_shape=[state_shape] + [VMEM((per, buses), f32)] * shared,
                input_output_aliases={4 + k: k for k in range(1 + shared)},
                compiler_params=params(2),
                name=f"ties_{iteration}",
            )(in_smem(row_of_tie), *tie_args, in_vmem(state), *[in_vmem(a) for a in made[2:]])
            state, sums = made[0], list(made[1:])
        else:
            state, parts, boundary = pl.pallas_call(
                tie_kernel,
                in_specs=[smem_spec] * 2 + [vmem_spec] * 5,
                out_specs=[vmem_spec] * 3,
                out_shape=[state_shape, parts_shape, VMEM((rows, 128), f32)],
                input_output_aliases={5: 0, 6: 1},
                compiler_params=params(2),
                name=f"ties_{iteration}",
            )(in_smem(row_of_tie), in_smem(send), *tie_args, in_vmem(state), in_vmem(parts))

    state = in_vmem(state)
    pieces = largest_divisor(blocks, 5)
    written = {}

    def multiply(chosen, totals):
        extra = [in_vmem(totals[k]) for k in chosen]
        written["mult"] = pl.pallas_call(
            functools.partial(multiplier_kernel, chosen, scen_all, pieces),
            in_specs=[vmem_spec] * (2 + len(extra)) + [any_spec],
            out_specs=any_spec,
            out_shape=whole,
            input_output_aliases={2 + len(extra): 0},
            scratch_shapes=[
                VMEM((len(chosen) * per, scenarios, buses), f32),
                pltpu.SemaphoreType.DMA((pieces,)),
            ],
            compiler_params=params(5),
            cost_estimate=cost(10**9, 10**6),
            name=f"multipliers_{chosen[0]}",
        )(state, in_vmem(multipliers), *extra, in_hbm(written["mult"]))
        return [in_hbm(written["mult"])]

    open_sections = list(range(shared))
    whole = pltpu.HBM((periods, scenarios, buses), f32)

    def write(turn, totals, ready):
        if turn == 0:
            own = list(range(shared, sections))
            written["dispatch"], written["mult"] = pl.pallas_call(
                functools.partial(output_kernel, own, scen_all, pieces),
                in_specs=[vmem_spec] * 2,
                out_specs=[any_spec] * 2,
                out_shape=[whole, whole],
                scratch_shapes=[
                    VMEM((periods, scenarios, buses), f32),
                    VMEM((len(own) * per, scenarios, buses), f32),
                    pltpu.SemaphoreType.DMA((2 * pieces,)),
                ],
                compiler_params=params(8),
                cost_estimate=cost(10**9, 10**6),
                name="outputs",
            )(state, in_vmem(multipliers))
            return [in_hbm(written["dispatch"])]
        if not ready:
            return []
        for k in ready:
            open_sections.remove(k)
        return multiply(ready, totals)

    totals = node_totals(sums, False, write)
    dispatch = written["dispatch"]
    new_mult = multiply(open_sections, totals)[0]
    return dispatch, new_mult


def solution(mesh):
    in_specs = (
        P(None, "scen", "area"),
        P(None, "scen", "area"),
        P(None, "area"),
        P(),
        P(None, "scen"),
        P("area", None, None, None),
        P("area", None),
        P("area"),
        P("area"),
        P("area"),
        P("area", None, None),
    )
    out_specs = (P(None, "scen", "area"), P(None, "scen", "area"))
    return jax.shard_map(local, mesh=mesh, in_specs=in_specs, out_specs=out_specs, check_vma=False)
```

```python
import functools

import jax
import jax.numpy as jnp
from jax import lax
from jax.experimental import pallas as pl
from jax.experimental.pallas import tpu as pltpu
from jax.sharding import PartitionSpec as P

STEPS = 8
step_size = 0.25
penalty = 1.0
keep = 1.0 - step_size * penalty

f32 = jnp.float32
bf16 = jnp.bfloat16
VMEM = pltpu.VMEM
SMEM = pltpu.SMEM
MIB = 1 << 20


def in_vmem(array):
    return pltpu.with_memory_space_constraint(array, VMEM)


def in_smem(array):
    return pltpu.with_memory_space_constraint(array, SMEM)


def in_hbm(array):
    return pltpu.with_memory_space_constraint(array, pltpu.HBM)


vmem_spec = pl.BlockSpec(memory_space=VMEM)
smem_spec = pl.BlockSpec(memory_space=SMEM)
any_spec = pl.BlockSpec(memory_space=pl.ANY)


def params(mib):
    return pltpu.CompilerParams(vmem_limit_bytes=mib * MIB)


def cost(flops, moved):
    return pl.CostEstimate(flops=flops, bytes_accessed=moved, transcendentals=0)


def split(value):
    high = value.astype(bf16)
    return high, (value - high.astype(f32)).astype(bf16)


def store_split(ref, index, value):
    rows = value.shape[0]
    high, low = split(value)
    ref[index, 0:rows] = high
    ref[index, rows : 2 * rows] = low


def fold(product, rows):
    return (product[:rows, :128] + product[:rows, 128:]) + (product[rows:, :128] + product[rows:, 128:])


def lanes(block):
    return pl.ds(pl.multiple_of(block * 128, 128), 128)


def partner(value, apart):
    rows = value.shape[0]
    up = pltpu.roll(value, rows - apart, 0)
    down = pltpu.roll(value, apart, 0)
    place = lax.broadcasted_iota(jnp.int32, value.shape, 0)
    return jnp.where((place & apart) == 0, up, down)


def local_mean(value, members):
    total, apart = value, 1
    while apart < members:
        total = total + partner(total, apart)
        apart *= 2
    return total * (1.0 / members)


def spread(ref, first, count, scenarios, block):
    shape = (count * scenarios, 128)
    place = lax.broadcasted_iota(jnp.int32, shape, 0)
    wide = jnp.broadcast_to(ref[first : first + 1, lanes(block)], shape)
    for t in range(1, count):
        row = jnp.broadcast_to(ref[first + t : first + t + 1, lanes(block)], shape)
        wide = jnp.where(place < t * scenarios, wide, row)
    return wide


def copies_of(pairs, sems):
    copies = [pltpu.make_async_copy(source, target, sems.at[n]) for n, (source, target) in enumerate(pairs)]
    for copy in copies:
        copy.start()
    return copies


def first_kernel(shared, per, small, send, start, *refs):
    sources, refs = refs[:small], refs[small:]
    places, sizes = places_of(shared, per)
    sums, targets = refs[: len(sizes)], refs[len(sizes) : len(sizes) + small]
    send_out, head, sems = refs[len(sizes) + small :]
    cuts = [pl.ds(k * per, per) for k in range(shared)]
    pairs = [(start.at[cut], head.at[cut]) for cut in cuts] + list(zip(sources, targets))
    copies = copies_of(pairs, sems)
    for k in range(shared):
        copies[k].wait()
        array, row = places[k]
        sums[array][row : row + per, 0 : head.shape[2]] = jnp.sum(head[k * per : (k + 1) * per], axis=1)
    send_out[0] = send[0]
    for copy in copies[shared:]:
        copy.wait()


def turns_of(levels):
    if levels < 3:
        return [[1 << level] for level in range(levels)]
    low = 1 << (levels - 2)
    return [[low, 2 * low, 3 * low]] + turns_of(levels - 2)


def swap(block, axis, apart):
    count = lax.axis_size(axis)
    return lax.ppermute(block, axis, [(i, i ^ apart) for i in range(count)])


def places_of(shared, per):
    groups, places, sizes = {}, [], []
    for k in range(shared):
        key = tuple(turns_of(shared - k)[0])
        if key not in groups:
            groups[key] = len(sizes)
            sizes.append(0)
        places.append((groups[key], sizes[groups[key]]))
        sizes[groups[key]] += per
    return places, sizes


def add_kernel(cuts, counts, *refs):
    inputs, outputs = iter(refs), refs[-len(counts) :]
    for cut, count, output in zip(cuts, counts, outputs):
        wide = slice(0, output.shape[1])
        total = next(inputs)[cut, wide]
        for _ in range(count):
            total = total + next(inputs)[cut, wide]
        output[...] = total


def node_totals(sums, shared, per, buses, beside):
    places, sizes = places_of(shared, per)
    totals = [sums[places[k][0]] for k in range(shared)]
    plans = [turns_of(shared - k) for k in range(shared)]
    for turn in range(max(len(plan) for plan in plans)):
        active = [k for k in range(shared) if turn < len(plans[k])]
        operands, cuts, received = [], [], {}
        for k in active:
            key = places[k][0] if turn == 0 else shared + k
            if key not in received:
                received[key] = [swap(totals[k], "scen", apart) for apart in plans[k][turn]]
            operands += [totals[k]] + received[key]
            cuts.append(slice(places[k][1], places[k][1] + per) if turn == 0 else slice(0, per))
        after = beside(turn, totals, [k for k in range(shared) if len(plans[k]) == turn])
        counts = [len(plans[k][turn]) for k in active]
        added = pl.pallas_call(
            functools.partial(add_kernel, cuts, counts),
            in_specs=[vmem_spec] * len(operands) + [any_spec] * len(after),
            out_specs=[vmem_spec] * len(active),
            out_shape=[VMEM((per, buses), f32) for k in active],
            compiler_params=params(2),
            name=f"node_add_{turn}",
        )(*[in_vmem(a) for a in operands], *after)
        for k, value in zip(active, added):
            totals[k] = value
    return totals


def from_pair(value, axis):
    count = lax.axis_size(axis)
    return lax.ppermute(value, axis, [(i, i ^ 1) for i in range(count)])


def from_other(value, axis):
    count = lax.axis_size(axis)
    return lax.ppermute(value, axis, [(i, (i + 1 if i % 2 else i - 1) % count) for i in range(count)])


def prepare_kernel(shared, per, scen_all, send, node_ids, load_factor,
                   start, mult, demand, tie_weight, state, parts, constant, ties, load, boundary):
    rows = state.shape[1]
    scenarios = start.shape[1]
    group = per * scenarios
    for k in range(node_ids.shape[1]):
        for s in range(scenarios):
            row = jnp.full((1, 128), load_factor[node_ids[s, k]], f32)
            for t in range(per):
                at = (k * per + t) * scenarios + s
                load[at : at + 1] = row
    boundary[...] = start[:, :, lanes(send[0])].reshape(boundary.shape)
    for m in range(tie_weight.shape[0]):
        high, low = split(tie_weight[m] * -step_size)
        for half in range(2):
            ties[m, half * 128 : (half + 1) * 128, 0:128] = high
            ties[m, half * 128 : (half + 1) * 128, 128:256] = low

    def one(i, carry):
        for k in range(rows // group):
            cut = slice(k * group, (k + 1) * group)
            span = slice(k * per, (k + 1) * per)
            x = start[span, :, lanes(i)].reshape(group, 128)
            m = mult[span, :, lanes(i)].reshape(group, 128)
            rest = m - spread(demand, k * per, per, scenarios, i) * load[cut]
            if k >= shared:
                rest = rest - penalty * local_mean(x, max(scen_all >> k, 1))
            constant[i, cut] = -step_size * rest
            state[i, cut] = x
        store_split(parts, i, state[i])
        return carry

    lax.fori_loop(0, state.shape[0], one, 0, unroll=largest_divisor(state.shape[0], 7))


def advance(i, other, weight, state, parts, constant, new_state, new_parts):
    left = jnp.concatenate([parts[i], parts[other]], axis=1)
    product = jnp.dot(left, weight, preferred_element_type=f32)
    value = (keep * state[i] + constant[i]) + fold(product, state.shape[1])
    new_state[i] = value
    store_split(new_parts, i, value)
    return value


def first_step(first, count, cols, values, state, parts, constant, weights, new_state, new_parts):
    for i in range(first, first + count):
        for j in range(2):
            high, low = split(values[i, j] * -step_size)
            weights[i, j * 128 : (j + 1) * 128, 0:128] = high
            weights[i, j * 128 : (j + 1) * 128, 128:256] = low
        advance(i, cols[1, i], weights[i], state, parts, constant, new_state, new_parts)


def first_step_begin(first, count, cols, values, state, parts, constant, after, *refs):
    first_step(first, count, cols, values, state, parts, constant, *refs)


def first_step_end(first, count, cols, values, state, parts, constant, after, w_in, s_in, p_in, *refs):
    first_step(first, count, cols, values, state, parts, constant, *refs)


def step_kernel(tie_row, cols, added, weights, constant, a, b, c, d, state, parts, new_state, new_parts):
    apply_ties(tie_row, added, state, parts)
    for i in range(state.shape[0]):
        advance(i, cols[1, i], weights[i], state, parts, constant, new_state, new_parts)


def add_sums(shared, per, scenarios, i, value, sums):
    group = per * scenarios
    for k, (array, row) in enumerate(places_of(shared, per)[0]):
        piece = value[k * group : (k + 1) * group].reshape(per, scenarios, 128)
        sums[array][row : row + per, lanes(i)] = jnp.sum(piece, axis=1)


def last_step_kernel(shared, per, scenarios, tie_row, cols, added, weights, constant, a, b, c, d,
                     state, parts, new_state, new_parts, *sums):
    apply_ties(tie_row, added, state, parts)
    for i in range(state.shape[0]):
        value = advance(i, cols[1, i], weights[i], state, parts, constant, new_state, new_parts)
        add_sums(shared, per, scenarios, i, value, sums)


def tie_products(tie_source, bound_count, other, pair, ties, left):
    for n, block in enumerate((other, pair)):
        high, low = split(block[...])
        left[n, :, 0:128] = high
        left[n, :, 128:256] = low
    partner_area = lax.axis_index("area") ^ 1
    products = []
    for m in range(ties.shape[0]):
        source = jnp.where(tie_source[m] // bound_count == partner_area, 1, 0)
        product = jnp.dot(left[source], ties[m], preferred_element_type=f32)
        products.append(product[:, :128] + product[:, 128:])
    return products


def meeting(row, tie_row, products):
    total = None
    for n, product in enumerate(products):
        term = jnp.where(tie_row[n] == row, 1.0, 0.0) * product
        total = term if total is None else total + term
    return total


def apply_ties(tie_row, added, state, parts):
    count = added.shape[0]
    products = [added[m] for m in range(count)]
    values = [state[tie_row[m]] + meeting(tie_row[m], tie_row, products) for m in range(count)]
    for m in range(count):
        state[tie_row[m]] = values[m]
        store_split(parts, tie_row[m], values[m])


def tie_kernel(tie_row, tie_source, send, pair, other, ties, state, added, boundary, left):
    products = tie_products(tie_source, send.shape[0], other, pair, ties, left)
    boundary[...] = state[send[0]] + meeting(send[0], tie_row, products)
    for m, product in enumerate(products):
        added[m] = product


def anchor_piece(k, scen_all, scenarios, total, i):
    mean = spread(total, 0, total.shape[0], scenarios, i) * (1.0 / (scen_all >> k))
    return (step_size * penalty) * mean


def first_tie_kernel(shared, scen_all, scenarios, tie_row, tie_source, send, pair, other, ties, state, *refs):
    totals = refs[:shared]
    added, boundary, left = refs[shared:]
    tie_kernel(tie_row, tie_source, send, pair, other, ties, state, added, boundary, left)
    group = totals[0].shape[0] * scenarios
    for k in range(shared):
        cut = slice(k * group, (k + 1) * group)
        boundary[cut] = boundary[cut] + anchor_piece(k, scen_all, scenarios, totals[k], send[0])


def anchor_kernel(shared, scen_all, scenarios, *refs):
    totals = refs[:shared]
    state, parts, constant = refs[shared + 3 :]
    rows = state.shape[1]
    group = totals[0].shape[0] * scenarios
    span = min(-(-shared * group // 16) * 16, rows)

    def one(i, carry):
        for k in range(shared):
            cut = slice(k * group, (k + 1) * group)
            mean = anchor_piece(k, scen_all, scenarios, totals[k], i)
            constant[i, cut] = constant[i, cut] + mean
            state[i, cut] = state[i, cut] + mean
        high_part, low_part = split(state[i, 0:span])
        parts[i, 0:span] = high_part
        parts[i, rows : rows + span] = low_part
        return carry

    lax.fori_loop(0, state.shape[0], one, 0, unroll=largest_divisor(state.shape[0], 14))


def last_tie_kernel(shared, per, scenarios, bound_count, tie_row, tie_source, pair, other, ties, *refs):
    left = refs[-1]
    half = (len(refs) - 1) // 2
    state, sums = refs[half], refs[half + 1 : -1]
    products = tie_products(tie_source, bound_count, other, pair, ties, left)
    count = len(products)
    values = [state[tie_row[m]] + meeting(tie_row[m], tie_row, products) for m in range(count)]
    for m in range(count):
        state[tie_row[m]] = values[m]
        add_sums(shared, per, scenarios, tie_row[m], values[m], sums)


def write_blocks(pieces, blocks, one, targets, sems):
    width = blocks // pieces
    copies = []
    for piece in range(pieces):
        lax.fori_loop(piece * width, (piece + 1) * width, one, 0, unroll=largest_divisor(width, 7))
        cut = pl.ds(piece * width * 128, width * 128)
        for buffer, out in targets:
            copies.append(pltpu.make_async_copy(buffer.at[:, :, cut], out.at[:, :, cut], sems.at[len(copies)]))
            copies[-1].start()
    for copy in copies:
        copy.wait()


def put_multipliers(chosen, scen_all, state, mult, totals, buffer, i):
    per, scenarios = buffer.shape[0] // len(chosen), buffer.shape[1]
    group = per * scenarios
    for n, k in enumerate(chosen):
        value = state[i, k * group : (k + 1) * group]
        if scen_all >> k > scenarios:
            mean = spread(totals[k], 0, per, scenarios, i) * (1.0 / (scen_all >> k))
        else:
            mean = local_mean(value, max(scen_all >> k, 1))
        gap = penalty * (value - mean)
        old = mult[k * per : (k + 1) * per, :, lanes(i)]
        buffer[n * per : (n + 1) * per, :, lanes(i)] = old + gap.reshape(per, scenarios, 128)


def output_kernel(chosen, scen_all, pieces, state, mult, dispatch, new_mult, whole, buffer, sems):
    periods, scenarios = whole.shape[:2]
    per = buffer.shape[0] // len(chosen)

    def one(i, carry):
        whole[:, :, lanes(i)] = state[i].reshape(periods, scenarios, 128)
        put_multipliers(chosen, scen_all, state, mult, {}, buffer, i)
        return carry

    rows = pl.ds(chosen[0] * per, len(chosen) * per)
    write_blocks(pieces, state.shape[0], one, [(whole, dispatch), (buffer, new_mult.at[rows])], sems)


def multiplier_kernel(chosen, scen_all, pieces, state, mult, *refs):
    new_mult, buffer, sems = refs[-3:]
    totals = dict(zip(chosen, refs[:-3]))
    per = buffer.shape[0] // len(chosen)

    def one(i, carry):
        put_multipliers(chosen, scen_all, state, mult, totals, buffer, i)
        return carry

    rows = pl.ds(chosen[0] * per, len(chosen) * per)
    write_blocks(pieces, state.shape[0], one, [(buffer, new_mult.at[rows])], sems)


def largest_divisor(count, most):
    return max(d for d in range(1, most + 1) if count % d == 0)


def local(
    start_dispatch,
    multipliers,
    demand,
    load_factor,
    node_ids,
    block_values,
    block_cols,
    send_block,
    tie_source,
    tie_row,
    tie_weight,
):
    periods, scenarios, buses = start_dispatch.shape
    blocks = buses // 128
    rows = periods * scenarios
    sections = node_ids.shape[0]
    per = periods // sections
    devices = lax.axis_size("scen")
    scen_all = scenarios * devices
    shared = devices.bit_length() - 1
    tie_count = tie_row.shape[0]

    small = [block_cols.T, tie_row, tie_source, node_ids.T, load_factor]
    padded = -(-buses // 1024) * 1024
    sum_shapes = [VMEM((size, padded if size > per else buses), f32) for size in places_of(shared, per)[1]]
    first = pl.pallas_call(
        functools.partial(first_kernel, shared, per, len(small)),
        in_specs=[smem_spec] + [any_spec] * (1 + len(small)),
        out_specs=[vmem_spec] * len(sum_shapes) + [smem_spec] * (len(small) + 1),
        out_shape=sum_shapes + [SMEM(a.shape, a.dtype) for a in small + [send_block]],
        scratch_shapes=[
            VMEM((shared * per, scenarios, buses), f32),
            pltpu.SemaphoreType.DMA((shared + len(small),)),
        ],
        compiler_params=params(4),
        cost_estimate=cost(2 * 10**10, 10**6),
        name="first_sums",
    )(send_block, in_hbm(start_dispatch), *[in_hbm(a) for a in small])
    sums = list(first[: len(sum_shapes)])
    cols, row_of_tie, source_of_tie, labels, factors, send = first[len(sum_shapes) :]

    state_shape = VMEM((blocks, rows, 128), f32)
    parts_shape = VMEM((blocks, 2 * rows, 128), bf16)

    weights_shape = VMEM((blocks, 256, 256), bf16)
    half = 2 * blocks // 7
    laid = {}

    def prepare(turn, totals, ready):
        after = totals[0]
        if turn == 0:
            laid["start"] = pl.pallas_call(
                functools.partial(prepare_kernel, shared, per, scen_all),
                in_specs=[smem_spec] * 3 + [vmem_spec] * 4,
                out_specs=[vmem_spec] * 6,
                out_shape=[state_shape, parts_shape, state_shape]
                + [VMEM((tie_count, 256, 256), bf16), VMEM((rows, 128), f32), VMEM((rows, 128), f32)],
                compiler_params=params(2),
                cost_estimate=cost(10**9, 10**6),
                name="prepare",
            )(in_smem(send), in_smem(labels), in_smem(factors),
              *[in_vmem(a) for a in (start_dispatch, multipliers, demand, tie_weight)])
        if turn > 1:
            return []
        first, count = (0, half) if turn == 0 else (half, blocks - half)
        held = [in_vmem(a) for a in laid["start"][:3]]
        made = [] if turn == 0 else [in_vmem(a) for a in laid["made"]]
        laid["made"] = pl.pallas_call(
            functools.partial(first_step_begin if turn == 0 else first_step_end, first, count),
            in_specs=[smem_spec] + [vmem_spec] * (5 + len(made)),
            out_specs=[vmem_spec] * 3,
            out_shape=[weights_shape, state_shape, parts_shape],
            input_output_aliases={} if turn == 0 else {6: 0, 7: 1, 8: 2},
            compiler_params=params(2),
            cost_estimate=cost(10**9, 10**6),
            name=f"step_0_{turn}",
        )(in_smem(cols), in_vmem(block_values), *held, in_vmem(after), *made)
        return [in_vmem(laid["made"][1])] if turn == 0 else []

    totals = node_totals(sums, shared, per, buses, prepare)
    if len(turns_of(shared)) < 2:
        prepare(1, totals, [])
    spare_state, spare_parts, constant, ties, load, boundary = laid["start"]
    weights, state, parts = laid["made"]
    added_shape = VMEM((tie_count, rows, 128), f32)
    left_shape = VMEM((2, rows, 256), bf16)
    tie_scalars = [in_smem(row_of_tie), in_smem(source_of_tie)]
    for iteration in range(STEPS):
        other = from_other(boundary, "area")
        pair = from_pair(boundary, "area")
        if iteration > 0:
            last = iteration == STEPS - 1
            made = pl.pallas_call(
                functools.partial(last_step_kernel, shared, per, scenarios) if last else step_kernel,
                in_specs=[smem_spec] * 2 + [vmem_spec] * 7,
                out_specs=[vmem_spec] * (4 + len(sum_shapes) * last),
                out_shape=[state_shape, parts_shape] * 2 + sum_shapes * last,
                input_output_aliases={5: 0, 6: 1, 7: 2, 8: 3},
                compiler_params=params(2),
                cost_estimate=cost(blocks * 2 * rows * 256 * 256 * 2, 12 * 10**6),
                name=f"step_{iteration}",
            )(tie_scalars[0], in_smem(cols),
              *[in_vmem(a) for a in (added, weights, constant, state, parts, spare_state, spare_parts)])
            spare_state, spare_parts, state, parts = made[:4]
            sums = list(made[4:])
        blocks_in = [in_vmem(pair), in_vmem(other), in_vmem(ties), in_vmem(state)]
        if iteration < STEPS - 1:
            nodes = [in_vmem(t) for t in totals] if iteration == 0 else []
            added, boundary = pl.pallas_call(
                functools.partial(first_tie_kernel, shared, scen_all, scenarios) if iteration == 0 else tie_kernel,
                in_specs=[smem_spec] * 3 + [vmem_spec] * (4 + len(nodes)),
                out_specs=[vmem_spec] * 2,
                out_shape=[added_shape, VMEM((rows, 128), f32)],
                scratch_shapes=[left_shape],
                compiler_params=params(2),
                name=f"ties_{iteration}",
            )(*tie_scalars, in_smem(send), *blocks_in, *nodes)
            if iteration == 0:
                state, parts, constant = pl.pallas_call(
                    functools.partial(anchor_kernel, shared, scen_all, scenarios),
                    in_specs=[vmem_spec] * (3 + shared),
                    out_specs=[vmem_spec] * 3,
                    out_shape=[state_shape, parts_shape, state_shape],
                    input_output_aliases={shared: 0, shared + 1: 1, shared + 2: 2},
                    compiler_params=params(2),
                    cost_estimate=cost(10**9, 10**6),
                    name="anchor",
                )(*nodes, in_vmem(state), in_vmem(parts), in_vmem(constant))
        else:
            made = pl.pallas_call(
                functools.partial(last_tie_kernel, shared, per, scenarios, send_block.shape[0]),
                in_specs=[smem_spec] * 2 + [vmem_spec] * (4 + len(sum_shapes)),
                out_specs=[vmem_spec] * (1 + len(sum_shapes)),
                out_shape=[state_shape] + sum_shapes,
                input_output_aliases={5 + k: k for k in range(1 + len(sum_shapes))},
                scratch_shapes=[left_shape],
                compiler_params=params(2),
                name=f"ties_{iteration}",
            )(*tie_scalars, *blocks_in, *[in_vmem(a) for a in sums])
            state, sums = made[0], list(made[1:])

    state = in_vmem(state)
    pieces = largest_divisor(blocks, 5)
    written = {}

    def multiply(chosen, totals):
        extra = [in_vmem(totals[k]) for k in chosen]
        written["mult"] = pl.pallas_call(
            functools.partial(multiplier_kernel, chosen, scen_all, pieces),
            in_specs=[vmem_spec] * (2 + len(extra)) + [any_spec],
            out_specs=any_spec,
            out_shape=whole,
            input_output_aliases={2 + len(extra): 0},
            scratch_shapes=[
                VMEM((len(chosen) * per, scenarios, buses), f32),
                pltpu.SemaphoreType.DMA((pieces,)),
            ],
            compiler_params=params(5),
            cost_estimate=cost(10**9, 10**6),
            name=f"multipliers_{chosen[0]}",
        )(state, in_vmem(multipliers), *extra, in_hbm(written["mult"]))
        return [in_hbm(written["mult"])]

    open_sections = list(range(shared))
    whole = pltpu.HBM((periods, scenarios, buses), f32)

    def write(turn, totals, ready):
        if turn == 0:
            own = list(range(shared, sections))
            written["dispatch"], written["mult"] = pl.pallas_call(
                functools.partial(output_kernel, own, scen_all, pieces),
                in_specs=[vmem_spec] * 2,
                out_specs=[any_spec] * 2,
                out_shape=[whole, whole],
                scratch_shapes=[
                    VMEM((periods, scenarios, buses), f32),
                    VMEM((len(own) * per, scenarios, buses), f32),
                    pltpu.SemaphoreType.DMA((2 * pieces,)),
                ],
                compiler_params=params(8),
                cost_estimate=cost(10**9, 10**6),
                name="outputs",
            )(state, in_vmem(multipliers))
            return [in_hbm(written["dispatch"])]
        if not ready:
            return []
        for k in ready:
            open_sections.remove(k)
        return multiply(ready, totals)

    totals = node_totals(sums, shared, per, buses, write)
    dispatch = written["dispatch"]
    new_mult = multiply(open_sections, totals)[0]
    return dispatch, new_mult


def solution(mesh):
    in_specs = (
        P(None, "scen", "area"),
        P(None, "scen", "area"),
        P(None, "area"),
        P(),
        P(None, "scen"),
        P("area", None, None, None),
        P("area", None),
        P("area"),
        P("area"),
        P("area"),
        P("area", None, None),
    )
    out_specs = (P(None, "scen", "area"), P(None, "scen", "area"))
    return jax.shard_map(local, mesh=mesh, in_specs=in_specs, out_specs=out_specs, check_vma=False)
```

```python
import functools

import jax
import jax.numpy as jnp
from jax import lax
from jax.experimental import pallas as pl
from jax.experimental.pallas import tpu as pltpu
from jax.sharding import PartitionSpec as P

STEPS = 8
step_size = 0.25
penalty = 1.0
keep = 1.0 - step_size * penalty

f32 = jnp.float32
bf16 = jnp.bfloat16
VMEM = pltpu.VMEM
SMEM = pltpu.SMEM
MIB = 1 << 20


def in_vmem(array):
    return pltpu.with_memory_space_constraint(array, VMEM)


def in_smem(array):
    return pltpu.with_memory_space_constraint(array, SMEM)


def in_hbm(array):
    return pltpu.with_memory_space_constraint(array, pltpu.HBM)


vmem_spec = pl.BlockSpec(memory_space=VMEM)
smem_spec = pl.BlockSpec(memory_space=SMEM)
any_spec = pl.BlockSpec(memory_space=pl.ANY)


def params(mib):
    return pltpu.CompilerParams(vmem_limit_bytes=mib * MIB)


def cost(flops, moved):
    return pl.CostEstimate(flops=flops, bytes_accessed=moved, transcendentals=0)


def split(value):
    high = value.astype(bf16)
    return high, (value - high.astype(f32)).astype(bf16)


def store_split(ref, index, value):
    rows = value.shape[0]
    high, low = split(value * -step_size)
    ref[index, 0:rows] = high
    ref[index, rows : 2 * rows] = low


def fold(product, rows):
    return (product[:rows, :128] + product[:rows, 128:]) + (product[rows:, :128] + product[rows:, 128:])


def lanes(block):
    return pl.ds(pl.multiple_of(block * 128, 128), 128)


def partner(value, apart):
    rows = value.shape[0]
    up = pltpu.roll(value, rows - apart, 0)
    down = pltpu.roll(value, apart, 0)
    place = lax.broadcasted_iota(jnp.int32, value.shape, 0)
    return jnp.where((place & apart) == 0, up, down)


def local_mean(value, members):
    total, apart = value, 1
    while apart < members:
        total = total + partner(total, apart)
        apart *= 2
    return total * (1.0 / members)


def spread(ref, first, count, scenarios, block):
    shape = (count * scenarios, 128)
    place = lax.broadcasted_iota(jnp.int32, shape, 0)
    wide = jnp.broadcast_to(ref[first : first + 1, lanes(block)], shape)
    for t in range(1, count):
        row = jnp.broadcast_to(ref[first + t : first + t + 1, lanes(block)], shape)
        wide = jnp.where(place < t * scenarios, wide, row)
    return wide


def copies_of(pairs, sems):
    copies = [pltpu.make_async_copy(source, target, sems.at[n]) for n, (source, target) in enumerate(pairs)]
    for copy in copies:
        copy.start()
    return copies


def first_kernel(shared, per, small, send, start, *refs):
    sources, refs = refs[:small], refs[small:]
    places, sizes = places_of(shared, per)
    sums, targets = refs[: len(sizes)], refs[len(sizes) : len(sizes) + small]
    send_out, head, sems = refs[len(sizes) + small :]
    cuts = [pl.ds(k * per, per) for k in range(shared)]
    pairs = [(start.at[cut], head.at[cut]) for cut in cuts] + list(zip(sources, targets))
    copies = copies_of(pairs, sems)
    for k in range(shared):
        copies[k].wait()
        array, row = places[k]
        sums[array][row : row + per, 0 : head.shape[2]] = jnp.sum(head[k * per : (k + 1) * per], axis=1)
    send_out[0] = send[0]
    for copy in copies[shared:]:
        copy.wait()


def turns_of(levels):
    if levels < 3:
        return [[1 << level] for level in range(levels)]
    low = 1 << (levels - 2)
    return [[low, 2 * low, 3 * low]] + turns_of(levels - 2)


def swap(block, axis, apart):
    count = lax.axis_size(axis)
    return lax.ppermute(block, axis, [(i, i ^ apart) for i in range(count)])


def places_of(shared, per):
    groups, places, sizes = {}, [], []
    for k in range(shared):
        key = tuple(turns_of(shared - k)[0])
        if key not in groups:
            groups[key] = len(sizes)
            sizes.append(0)
        places.append((groups[key], sizes[groups[key]]))
        sizes[groups[key]] += per
    return places, sizes


def add_kernel(cuts, counts, *refs):
    inputs, outputs = iter(refs), refs[-len(counts) :]
    for cut, count, output in zip(cuts, counts, outputs):
        wide = slice(0, output.shape[1])
        total = next(inputs)[cut, wide]
        for _ in range(count):
            total = total + next(inputs)[cut, wide]
        output[...] = total


def node_totals(sums, shared, per, buses, beside):
    places, sizes = places_of(shared, per)
    totals = [sums[places[k][0]] for k in range(shared)]
    plans = [turns_of(shared - k) for k in range(shared)]
    for turn in range(max(len(plan) for plan in plans)):
        active = [k for k in range(shared) if turn < len(plans[k])]
        operands, cuts, received = [], [], {}
        for k in active:
            key = places[k][0] if turn == 0 else shared + k
            if key not in received:
                received[key] = [swap(totals[k], "scen", apart) for apart in plans[k][turn]]
            operands += [totals[k]] + received[key]
            cuts.append(slice(places[k][1], places[k][1] + per) if turn == 0 else slice(0, per))
        after = beside(turn, totals, [k for k in range(shared) if len(plans[k]) == turn])
        counts = [len(plans[k][turn]) for k in active]
        added = pl.pallas_call(
            functools.partial(add_kernel, cuts, counts),
            in_specs=[vmem_spec] * len(operands) + [any_spec] * len(after),
            out_specs=[vmem_spec] * len(active),
            out_shape=[VMEM((per, buses), f32) for k in active],
            compiler_params=params(2),
            name=f"node_add_{turn}",
        )(*[in_vmem(a) for a in operands], *after)
        for k, value in zip(active, added):
            totals[k] = value
    return totals


def from_pair(value, axis):
    count = lax.axis_size(axis)
    return lax.ppermute(value, axis, [(i, i ^ 1) for i in range(count)])


def from_other(value, axis):
    count = lax.axis_size(axis)
    return lax.ppermute(value, axis, [(i, (i + 1 if i % 2 else i - 1) % count) for i in range(count)])


def prepare_kernel(shared, per, scen_all, send, tie_row, tie_source, node_ids, load_factor,
                   start, mult, demand, tie_weight, state, parts, constant, ties, loops, load, boundary):
    rows = state.shape[1]
    scenarios = start.shape[1]
    group = per * scenarios
    for k in range(node_ids.shape[1]):
        for s in range(scenarios):
            row = jnp.full((1, 128), load_factor[node_ids[s, k]], f32)
            for t in range(per):
                at = (k * per + t) * scenarios + s
                load[at : at + 1] = row
    boundary[...] = start[:, :, lanes(send[0])].reshape(boundary.shape)
    def put_matrix(ref, n, value):
        high, low = split(value)
        for half in range(2):
            ref[n, half * 128 : (half + 1) * 128, 0:128] = high
            ref[n, half * 128 : (half + 1) * 128, 128:256] = low

    partner_area = lax.axis_index("area") ^ 1
    ending = [jnp.zeros((128, 128), f32)] * 2
    for m in range(tie_weight.shape[0]):
        value = tie_weight[m] * -step_size
        put_matrix(ties, m, value)
        ends = tie_row[m] == send[0]
        paired = tie_source[m] // send.shape[0] == partner_area
        ending[0] = ending[0] + jnp.where(jnp.logical_and(ends, jnp.logical_not(paired)), 1.0, 0.0) * value
        ending[1] = ending[1] + jnp.where(jnp.logical_and(ends, paired), 1.0, 0.0) * value
    for n in range(2):
        put_matrix(loops, n, ending[n])

    def one(i, carry):
        for k in range(rows // group):
            cut = slice(k * group, (k + 1) * group)
            span = slice(k * per, (k + 1) * per)
            x = start[span, :, lanes(i)].reshape(group, 128)
            m = mult[span, :, lanes(i)].reshape(group, 128)
            rest = m - spread(demand, k * per, per, scenarios, i) * load[cut]
            if k >= shared:
                rest = rest - penalty * local_mean(x, max(scen_all >> k, 1))
            constant[i, cut] = -step_size * rest
            state[i, cut] = x
        store_split(parts, i, state[i])
        return carry

    lax.fori_loop(0, state.shape[0], one, 0, unroll=largest_divisor(state.shape[0], 7))


def advance(i, other, weight, state, parts, constant, new_state, new_parts):
    left = jnp.concatenate([parts[i], parts[other]], axis=1)
    product = jnp.dot(left, weight, preferred_element_type=f32)
    value = (keep * state[i] + constant[i]) + fold(product, state.shape[1])
    new_state[i] = value
    store_split(new_parts, i, value)
    return value


def first_step(first, count, cols, values, state, parts, constant, weights, new_state, new_parts):
    for i in range(first, first + count):
        for j in range(2):
            high, low = split(values[i, j])
            weights[i, j * 128 : (j + 1) * 128, 0:128] = high
            weights[i, j * 128 : (j + 1) * 128, 128:256] = low
        advance(i, cols[1, i], weights[i], state, parts, constant, new_state, new_parts)


def first_step_begin(first, count, cols, values, state, parts, constant, after, *refs):
    first_step(first, count, cols, values, state, parts, constant, *refs)


def first_step_end(first, count, cols, values, state, parts, constant, after, w_in, s_in, p_in, *refs):
    first_step(first, count, cols, values, state, parts, constant, *refs)


def step_kernel(tie_row, tie_source, cols, bound_count, other, pair, ties, weights, constant, a, b, c, d,
                state, parts, new_state, new_parts, left):
    products = tie_products(tie_source, bound_count, other, pair, ties, left)
    apply_ties(tie_row, products, state, parts)
    for i in range(state.shape[0]):
        advance(i, cols[1, i], weights[i], state, parts, constant, new_state, new_parts)


def add_sums(shared, per, scenarios, i, value, sums):
    group = per * scenarios
    for k, (array, row) in enumerate(places_of(shared, per)[0]):
        piece = value[k * group : (k + 1) * group].reshape(per, scenarios, 128)
        sums[array][row : row + per, lanes(i)] = jnp.sum(piece, axis=1)


def last_step_kernel(shared, per, scenarios, tie_row, tie_source, cols, bound_count, other, pair, ties,
                     weights, constant, a, b, c, d, state, parts, new_state, new_parts, *refs):
    sums, left = refs[:-1], refs[-1]
    products = tie_products(tie_source, bound_count, other, pair, ties, left)
    apply_ties(tie_row, products, state, parts)
    for i in range(state.shape[0]):
        value = advance(i, cols[1, i], weights[i], state, parts, constant, new_state, new_parts)
        add_sums(shared, per, scenarios, i, value, sums)


def tie_products(tie_source, bound_count, other, pair, ties, left):
    for n, block in enumerate((other, pair)):
        high, low = split(block[...])
        left[n, :, 0:128] = high
        left[n, :, 128:256] = low
    partner_area = lax.axis_index("area") ^ 1
    products = []
    for m in range(ties.shape[0]):
        source = jnp.where(tie_source[m] // bound_count[0] == partner_area, 1, 0)
        product = jnp.dot(left[source], ties[m], preferred_element_type=f32)
        products.append(product[:, :128] + product[:, 128:])
    return products


def meeting(row, tie_row, products):
    total = None
    for n, product in enumerate(products):
        term = jnp.where(tie_row[n] == row, 1.0, 0.0) * product
        total = term if total is None else total + term
    return total


def apply_ties(tie_row, products, state, parts):
    count = len(products)
    values = [state[tie_row[m]] + meeting(tie_row[m], tie_row, products) for m in range(count)]
    for m in range(count):
        state[tie_row[m]] = values[m]
        store_split(parts, tie_row[m], values[m])


def boundary_after(send, other, pair, loops, state):
    value = state[send[0]]
    for n, block in enumerate((other, pair)):
        left = jnp.concatenate(split(block[...]), axis=1)
        product = jnp.dot(left, loops[n], preferred_element_type=f32)
        value = value + (product[:, :128] + product[:, 128:])
    return value


def tie_kernel(send, pair, other, loops, state, boundary):
    boundary[...] = boundary_after(send, other, pair, loops, state)


def anchor_piece(k, scen_all, scenarios, total, i):
    mean = spread(total, 0, total.shape[0], scenarios, i) * (1.0 / (scen_all >> k))
    return (step_size * penalty) * mean


def first_tie_kernel(shared, scen_all, scenarios, send, pair, other, loops, state, *refs):
    totals, boundary = refs[:shared], refs[shared]
    boundary[...] = boundary_after(send, other, pair, loops, state)
    group = totals[0].shape[0] * scenarios
    for k in range(shared):
        cut = slice(k * group, (k + 1) * group)
        boundary[cut] = boundary[cut] + anchor_piece(k, scen_all, scenarios, totals[k], send[0])


def anchor_kernel(shared, scen_all, scenarios, *refs):
    totals = refs[:shared]
    state, parts, constant = refs[shared + 3 :]
    rows = state.shape[1]
    group = totals[0].shape[0] * scenarios
    span = min(-(-shared * group // 16) * 16, rows)

    def one(i, carry):
        for k in range(shared):
            cut = slice(k * group, (k + 1) * group)
            mean = anchor_piece(k, scen_all, scenarios, totals[k], i)
            constant[i, cut] = constant[i, cut] + mean
            state[i, cut] = state[i, cut] + mean
        high_part, low_part = split(state[i, 0:span] * -step_size)
        parts[i, 0:span] = high_part
        parts[i, rows : rows + span] = low_part
        return carry

    lax.fori_loop(0, state.shape[0], one, 0, unroll=largest_divisor(state.shape[0], 14))


def last_tie_kernel(shared, per, scenarios, bound_count, tie_row, tie_source, pair, other, ties, *refs):
    left = refs[-1]
    half = (len(refs) - 1) // 2
    state, sums = refs[half], refs[half + 1 : -1]
    products = tie_products(tie_source, bound_count, other, pair, ties, left)
    count = len(products)
    values = [state[tie_row[m]] + meeting(tie_row[m], tie_row, products) for m in range(count)]
    for m in range(count):
        state[tie_row[m]] = values[m]
        add_sums(shared, per, scenarios, tie_row[m], values[m], sums)


def write_blocks(pieces, blocks, one, targets, sems):
    width = blocks // pieces
    copies = []
    for piece in range(pieces):
        lax.fori_loop(piece * width, (piece + 1) * width, one, 0, unroll=largest_divisor(width, 7))
        cut = pl.ds(piece * width * 128, width * 128)
        for buffer, out in targets:
            copies.append(pltpu.make_async_copy(buffer.at[:, :, cut], out.at[:, :, cut], sems.at[len(copies)]))
            copies[-1].start()
    for copy in copies:
        copy.wait()


def put_multipliers(chosen, scen_all, state, mult, totals, buffer, i):
    per, scenarios = buffer.shape[0] // len(chosen), buffer.shape[1]
    group = per * scenarios
    for n, k in enumerate(chosen):
        value = state[i, k * group : (k + 1) * group]
        if scen_all >> k > scenarios:
            mean = spread(totals[k], 0, per, scenarios, i) * (1.0 / (scen_all >> k))
        else:
            mean = local_mean(value, max(scen_all >> k, 1))
        gap = penalty * (value - mean)
        old = mult[k * per : (k + 1) * per, :, lanes(i)]
        buffer[n * per : (n + 1) * per, :, lanes(i)] = old + gap.reshape(per, scenarios, 128)


def output_kernel(chosen, scen_all, pieces, state, mult, dispatch, new_mult, whole, buffer, sems):
    periods, scenarios = whole.shape[:2]
    per = buffer.shape[0] // len(chosen)

    def one(i, carry):
        whole[:, :, lanes(i)] = state[i].reshape(periods, scenarios, 128)
        put_multipliers(chosen, scen_all, state, mult, {}, buffer, i)
        return carry

    rows = pl.ds(chosen[0] * per, len(chosen) * per)
    write_blocks(pieces, state.shape[0], one, [(whole, dispatch), (buffer, new_mult.at[rows])], sems)


def multiplier_kernel(chosen, scen_all, pieces, state, mult, *refs):
    new_mult, buffer, sems = refs[-3:]
    totals = dict(zip(chosen, refs[:-3]))
    per = buffer.shape[0] // len(chosen)

    def one(i, carry):
        put_multipliers(chosen, scen_all, state, mult, totals, buffer, i)
        return carry

    rows = pl.ds(chosen[0] * per, len(chosen) * per)
    write_blocks(pieces, state.shape[0], one, [(buffer, new_mult.at[rows])], sems)


def largest_divisor(count, most):
    return max(d for d in range(1, most + 1) if count % d == 0)


def local(
    start_dispatch,
    multipliers,
    demand,
    load_factor,
    node_ids,
    block_values,
    block_cols,
    send_block,
    tie_source,
    tie_row,
    tie_weight,
):
    periods, scenarios, buses = start_dispatch.shape
    blocks = buses // 128
    rows = periods * scenarios
    sections = node_ids.shape[0]
    per = periods // sections
    devices = lax.axis_size("scen")
    scen_all = scenarios * devices
    shared = devices.bit_length() - 1
    tie_count = tie_row.shape[0]

    small = [block_cols.T, tie_row, tie_source, node_ids.T, load_factor]
    padded = -(-buses // 1024) * 1024
    sum_shapes = [VMEM((size, padded if size > per else buses), f32) for size in places_of(shared, per)[1]]
    first = pl.pallas_call(
        functools.partial(first_kernel, shared, per, len(small)),
        in_specs=[smem_spec] + [any_spec] * (1 + len(small)),
        out_specs=[vmem_spec] * len(sum_shapes) + [smem_spec] * (len(small) + 1),
        out_shape=sum_shapes + [SMEM(a.shape, a.dtype) for a in small + [send_block]],
        scratch_shapes=[
            VMEM((shared * per, scenarios, buses), f32),
            pltpu.SemaphoreType.DMA((shared + len(small),)),
        ],
        compiler_params=params(4),
        cost_estimate=cost(2 * 10**10, 10**6),
        name="first_sums",
    )(send_block, in_hbm(start_dispatch), *[in_hbm(a) for a in small])
    sums = list(first[: len(sum_shapes)])
    cols, row_of_tie, source_of_tie, labels, factors, send = first[len(sum_shapes) :]

    state_shape = VMEM((blocks, rows, 128), f32)
    parts_shape = VMEM((blocks, 2 * rows, 128), bf16)

    weights_shape = VMEM((blocks, 256, 256), bf16)
    half = blocks // 7
    laid = {}

    def prepare(turn, totals, ready):
        after = totals[0]
        if turn == 0:
            laid["start"] = pl.pallas_call(
                functools.partial(prepare_kernel, shared, per, scen_all),
                in_specs=[smem_spec] * 5 + [vmem_spec] * 4,
                out_specs=[vmem_spec] * 7,
                out_shape=[state_shape, parts_shape, state_shape]
                + [VMEM((tie_count, 256, 256), bf16), VMEM((2, 256, 256), bf16)]
                + [VMEM((rows, 128), f32), VMEM((rows, 128), f32)],
                compiler_params=params(2),
                cost_estimate=cost(10**9, 10**6),
                name="prepare",
            )(in_smem(send), in_smem(row_of_tie), in_smem(source_of_tie), in_smem(labels), in_smem(factors),
              *[in_vmem(a) for a in (start_dispatch, multipliers, demand, tie_weight)])
        if turn > 1:
            return []
        first, count = (0, half) if turn == 0 else (half, blocks - half)
        held = [in_vmem(a) for a in laid["start"][:3]]
        made = [] if turn == 0 else [in_vmem(a) for a in laid["made"]]
        laid["made"] = pl.pallas_call(
            functools.partial(first_step_begin if turn == 0 else first_step_end, first, count),
            in_specs=[smem_spec] + [vmem_spec] * (5 + len(made)),
            out_specs=[vmem_spec] * 3,
            out_shape=[weights_shape, state_shape, parts_shape],
            input_output_aliases={} if turn == 0 else {6: 0, 7: 1, 8: 2},
            compiler_params=params(2),
            cost_estimate=cost(10**9, 10**6),
            name=f"step_0_{turn}",
        )(in_smem(cols), in_vmem(block_values), *held, in_vmem(after), *made)
        return [in_vmem(laid["made"][1])] if turn == 0 else []

    totals = node_totals(sums, shared, per, buses, prepare)
    if len(turns_of(shared)) < 2:
        prepare(1, totals, [])
    spare_state, spare_parts, constant, ties, loops, load, boundary = laid["start"]
    weights, state, parts = laid["made"]
    left_shape = VMEM((2, rows, 256), bf16)
    tie_scalars = [in_smem(row_of_tie), in_smem(source_of_tie)]
    bound_count = send_block.shape[0]
    for iteration in range(STEPS):
        previous = (other, pair) if iteration > 0 else None
        other = from_other(boundary, "area")
        pair = from_pair(boundary, "area")
        if iteration > 0:
            last = iteration == STEPS - 1
            body = functools.partial(last_step_kernel, shared, per, scenarios) if last else step_kernel

            def kernel(tie_row, tie_source, cols, *refs, body=body):
                body(tie_row, tie_source, cols, (bound_count,), *refs)

            made = pl.pallas_call(
                kernel,
                in_specs=[smem_spec] * 3 + [vmem_spec] * 9,
                out_specs=[vmem_spec] * (4 + len(sum_shapes) * last),
                out_shape=[state_shape, parts_shape] * 2 + sum_shapes * last,
                input_output_aliases={8: 0, 9: 1, 10: 2, 11: 3},
                scratch_shapes=[left_shape],
                compiler_params=params(2),
                cost_estimate=cost(blocks * 2 * rows * 256 * 256 * 2, 12 * 10**6),
                name=f"step_{iteration}",
            )(*tie_scalars, in_smem(cols), *[in_vmem(a) for a in previous],
              *[in_vmem(a) for a in (ties, weights, constant, state, parts, spare_state, spare_parts)])
            spare_state, spare_parts, state, parts = made[:4]
            sums = list(made[4:])
        arrived = [in_vmem(pair), in_vmem(other)]
        if iteration < STEPS - 1:
            nodes = [in_vmem(t) for t in totals] if iteration == 0 else []
            (boundary,) = pl.pallas_call(
                functools.partial(first_tie_kernel, shared, scen_all, scenarios) if iteration == 0 else tie_kernel,
                in_specs=[smem_spec] + [vmem_spec] * (4 + len(nodes)),
                out_specs=[vmem_spec],
                out_shape=[VMEM((rows, 128), f32)],
                compiler_params=params(2),
                name=f"ties_{iteration}",
            )(in_smem(send), *arrived, in_vmem(loops), in_vmem(state), *nodes)
            if iteration == 0:
                state, parts, constant = pl.pallas_call(
                    functools.partial(anchor_kernel, shared, scen_all, scenarios),
                    in_specs=[vmem_spec] * (3 + shared),
                    out_specs=[vmem_spec] * 3,
                    out_shape=[state_shape, parts_shape, state_shape],
                    input_output_aliases={shared: 0, shared + 1: 1, shared + 2: 2},
                    compiler_params=params(2),
                    cost_estimate=cost(10**9, 10**6),
                    name="anchor",
                )(*nodes, in_vmem(state), in_vmem(parts), in_vmem(constant))
        else:
            made = pl.pallas_call(
                functools.partial(last_tie_kernel, shared, per, scenarios, (bound_count,)),
                in_specs=[smem_spec] * 2 + [vmem_spec] * (4 + len(sum_shapes)),
                out_specs=[vmem_spec] * (1 + len(sum_shapes)),
                out_shape=[state_shape] + sum_shapes,
                input_output_aliases={5 + k: k for k in range(1 + len(sum_shapes))},
                scratch_shapes=[left_shape],
                compiler_params=params(2),
                name=f"ties_{iteration}",
            )(*tie_scalars, *arrived, in_vmem(ties), in_vmem(state), *[in_vmem(a) for a in sums])
            state, sums = made[0], list(made[1:])

    state = in_vmem(state)
    pieces = largest_divisor(blocks, 5)
    written = {}

    def multiply(chosen, totals):
        extra = [in_vmem(totals[k]) for k in chosen]
        written["mult"] = pl.pallas_call(
            functools.partial(multiplier_kernel, chosen, scen_all, pieces),
            in_specs=[vmem_spec] * (2 + len(extra)) + [any_spec],
            out_specs=any_spec,
            out_shape=whole,
            input_output_aliases={2 + len(extra): 0},
            scratch_shapes=[
                VMEM((len(chosen) * per, scenarios, buses), f32),
                pltpu.SemaphoreType.DMA((pieces,)),
            ],
            compiler_params=params(5),
            cost_estimate=cost(10**9, 10**6),
            name=f"multipliers_{chosen[0]}",
        )(state, in_vmem(multipliers), *extra, in_hbm(written["mult"]))
        return [in_hbm(written["mult"])]

    open_sections = list(range(shared))
    whole = pltpu.HBM((periods, scenarios, buses), f32)

    def write(turn, totals, ready):
        if turn == 0:
            own = list(range(shared, sections))
            written["dispatch"], written["mult"] = pl.pallas_call(
                functools.partial(output_kernel, own, scen_all, pieces),
                in_specs=[vmem_spec] * 2,
                out_specs=[any_spec] * 2,
                out_shape=[whole, whole],
                scratch_shapes=[
                    VMEM((periods, scenarios, buses), f32),
                    VMEM((len(own) * per, scenarios, buses), f32),
                    pltpu.SemaphoreType.DMA((2 * pieces,)),
                ],
                compiler_params=params(8),
                cost_estimate=cost(10**9, 10**6),
                name="outputs",
            )(state, in_vmem(multipliers))
            return [in_hbm(written["dispatch"])]
        if not ready:
            return []
        for k in ready:
            open_sections.remove(k)
        return multiply(ready, totals)

    totals = node_totals(sums, shared, per, buses, write)
    dispatch = written["dispatch"]
    new_mult = multiply(open_sections, totals)[0]
    return dispatch, new_mult


def solution(mesh):
    in_specs = (
        P(None, "scen", "area"),
        P(None, "scen", "area"),
        P(None, "area"),
        P(),
        P(None, "scen"),
        P("area", None, None, None),
        P("area", None),
        P("area"),
        P("area"),
        P("area"),
        P("area", None, None),
    )
    out_specs = (P(None, "scen", "area"), P(None, "scen", "area"))
    return jax.shard_map(local, mesh=mesh, in_specs=in_specs, out_specs=out_specs, check_vma=False)
```

```python
import functools

import jax
import jax.numpy as jnp
from jax import lax
from jax.experimental import pallas as pl
from jax.experimental.pallas import tpu as pltpu
from jax.sharding import PartitionSpec as P

STEPS = 8
step_size = 0.25
penalty = 1.0
keep = 1.0 - step_size * penalty

f32 = jnp.float32
bf16 = jnp.bfloat16
VMEM = pltpu.VMEM
SMEM = pltpu.SMEM
MIB = 1 << 20


def in_vmem(array):
    return pltpu.with_memory_space_constraint(array, VMEM)


def in_smem(array):
    return pltpu.with_memory_space_constraint(array, SMEM)


def in_hbm(array):
    return pltpu.with_memory_space_constraint(array, pltpu.HBM)


vmem_spec = pl.BlockSpec(memory_space=VMEM)
smem_spec = pl.BlockSpec(memory_space=SMEM)
any_spec = pl.BlockSpec(memory_space=pl.ANY)


def params(mib):
    return pltpu.CompilerParams(vmem_limit_bytes=mib * MIB)


def cost(flops, moved):
    return pl.CostEstimate(flops=flops, bytes_accessed=moved, transcendentals=0)


def split(value):
    high = value.astype(bf16)
    return high, (value - high.astype(f32)).astype(bf16)


def store_split(ref, index, value):
    rows = value.shape[0]
    high, low = split(value * -step_size)
    ref[index, 0:rows] = high
    ref[index, rows : 2 * rows] = low


def fold(product, rows):
    return (product[:rows, :128] + product[:rows, 128:]) + (product[rows:, :128] + product[rows:, 128:])


def lanes(block):
    return pl.ds(pl.multiple_of(block * 128, 128), 128)


def partner(value, apart):
    rows = value.shape[0]
    up = pltpu.roll(value, rows - apart, 0)
    down = pltpu.roll(value, apart, 0)
    place = lax.broadcasted_iota(jnp.int32, value.shape, 0)
    return jnp.where((place & apart) == 0, up, down)


def local_mean(value, members):
    total, apart = value, 1
    while apart < members:
        total = total + partner(total, apart)
        apart *= 2
    return total * (1.0 / members)


def spread(ref, first, count, scenarios, block):
    shape = (count * scenarios, 128)
    place = lax.broadcasted_iota(jnp.int32, shape, 0)
    wide = jnp.broadcast_to(ref[first : first + 1, lanes(block)], shape)
    for t in range(1, count):
        row = jnp.broadcast_to(ref[first + t : first + t + 1, lanes(block)], shape)
        wide = jnp.where(place < t * scenarios, wide, row)
    return wide


def copies_of(pairs, sems):
    copies = [pltpu.make_async_copy(source, target, sems.at[n]) for n, (source, target) in enumerate(pairs)]
    for copy in copies:
        copy.start()
    return copies


def first_kernel(shared, per, small, send, start, *refs):
    sources, refs = refs[:small], refs[small:]
    places, sizes = places_of(shared, per)
    sums, targets = refs[: len(sizes)], refs[len(sizes) : len(sizes) + small]
    send_out, head, sems = refs[len(sizes) + small :]
    cuts = [pl.ds(k * per, per) for k in range(shared)]
    pairs = [(start.at[cut], head.at[cut]) for cut in cuts] + list(zip(sources, targets))
    copies = copies_of(pairs, sems)
    for k in range(shared):
        copies[k].wait()
        array, row = places[k]
        sums[array][row : row + per, 0 : head.shape[2]] = jnp.sum(head[k * per : (k + 1) * per], axis=1)
    send_out[0] = send[0]
    for copy in copies[shared:]:
        copy.wait()


def turns_of(levels):
    if levels < 3:
        return [[1 << level] for level in range(levels)]
    low = 1 << (levels - 2)
    return [[low, 2 * low, 3 * low]] + turns_of(levels - 2)


def swap(block, axis, apart):
    count = lax.axis_size(axis)
    return lax.ppermute(block, axis, [(i, i ^ apart) for i in range(count)])


def places_of(shared, per):
    groups, places, sizes = {}, [], []
    for k in range(shared):
        key = tuple(turns_of(shared - k)[0])
        if key not in groups:
            groups[key] = len(sizes)
            sizes.append(0)
        places.append((groups[key], sizes[groups[key]]))
        sizes[groups[key]] += per
    return places, sizes


def add_kernel(cuts, counts, *refs):
    inputs, outputs = iter(refs), refs[-len(counts) :]
    for cut, count, output in zip(cuts, counts, outputs):
        wide = slice(0, output.shape[1])
        total = next(inputs)[cut, wide]
        for _ in range(count):
            total = total + next(inputs)[cut, wide]
        output[...] = total


def node_totals(sums, shared, per, buses, beside):
    places, sizes = places_of(shared, per)
    totals = [sums[places[k][0]] for k in range(shared)]
    plans = [turns_of(shared - k) for k in range(shared)]
    for turn in range(max(len(plan) for plan in plans)):
        active = [k for k in range(shared) if turn < len(plans[k])]
        operands, cuts, received = [], [], {}
        for k in active:
            key = places[k][0] if turn == 0 else shared + k
            if key not in received:
                received[key] = [swap(totals[k], "scen", apart) for apart in plans[k][turn]]
            operands += [totals[k]] + received[key]
            cuts.append(slice(places[k][1], places[k][1] + per) if turn == 0 else slice(0, per))
        after = beside(turn, totals, [k for k in range(shared) if len(plans[k]) == turn])
        counts = [len(plans[k][turn]) for k in active]
        added = pl.pallas_call(
            functools.partial(add_kernel, cuts, counts),
            in_specs=[vmem_spec] * len(operands) + [any_spec] * len(after),
            out_specs=[vmem_spec] * len(active),
            out_shape=[VMEM((per, buses), f32) for k in active],
            compiler_params=params(2),
            name=f"node_add_{turn}",
        )(*[in_vmem(a) for a in operands], *after)
        for k, value in zip(active, added):
            totals[k] = value
    return totals


def from_pair(value, axis):
    count = lax.axis_size(axis)
    return lax.ppermute(value, axis, [(i, i ^ 1) for i in range(count)])


def from_other(value, axis):
    count = lax.axis_size(axis)
    return lax.ppermute(value, axis, [(i, (i + 1 if i % 2 else i - 1) % count) for i in range(count)])


def prepare_kernel(shared, per, scen_all, send, tie_row, tie_source, node_ids, load_factor,
                   start, mult, demand, tie_weight, state, parts, constant, ties, loops, load, boundary):
    rows = state.shape[1]
    scenarios = start.shape[1]
    group = per * scenarios
    for k in range(node_ids.shape[1]):
        for s in range(scenarios):
            row = jnp.full((1, 128), load_factor[node_ids[s, k]], f32)
            for t in range(per):
                at = (k * per + t) * scenarios + s
                load[at : at + 1] = row
    boundary[...] = start[:, :, lanes(send[0])].reshape(boundary.shape)
    def put_matrix(ref, n, value):
        high, low = split(value)
        for half in range(2):
            ref[n, half * 128 : (half + 1) * 128, 0:128] = high
            ref[n, half * 128 : (half + 1) * 128, 128:256] = low

    partner_area = lax.axis_index("area") ^ 1
    ending = [jnp.zeros((128, 128), f32)] * 2
    for m in range(tie_weight.shape[0]):
        value = tie_weight[m] * -step_size
        put_matrix(ties, m, value)
        ends = tie_row[m] == send[0]
        paired = tie_source[m] // send.shape[0] == partner_area
        ending[0] = ending[0] + jnp.where(jnp.logical_and(ends, jnp.logical_not(paired)), 1.0, 0.0) * value
        ending[1] = ending[1] + jnp.where(jnp.logical_and(ends, paired), 1.0, 0.0) * value
    for n in range(2):
        put_matrix(loops, n, ending[n])

    def one(i, carry):
        for k in range(rows // group):
            cut = slice(k * group, (k + 1) * group)
            span = slice(k * per, (k + 1) * per)
            x = start[span, :, lanes(i)].reshape(group, 128)
            m = mult[span, :, lanes(i)].reshape(group, 128)
            rest = m - spread(demand, k * per, per, scenarios, i) * load[cut]
            if k >= shared:
                rest = rest - penalty * local_mean(x, max(scen_all >> k, 1))
            constant[i, cut] = -step_size * rest
            state[i, cut] = x
        store_split(parts, i, state[i])
        return carry

    lax.fori_loop(0, state.shape[0], one, 0, unroll=largest_divisor(state.shape[0], 7))


def advance(i, other, weight, state, parts, constant, new_state, new_parts):
    left = jnp.concatenate([parts[i], parts[other]], axis=1)
    product = jnp.dot(left, weight, preferred_element_type=f32)
    value = (keep * state[i] + constant[i]) + fold(product, state.shape[1])
    new_state[i] = value
    store_split(new_parts, i, value)
    return value


def first_step_kernel(cols, values, state, parts, constant, after, weights, new_state, new_parts):
    for i in range(state.shape[0]):
        weight = jnp.concatenate([jnp.concatenate(split(values[i, j]), axis=1) for j in range(2)], axis=0)
        weights[i] = weight
        advance(i, cols[1, i], weight, state, parts, constant, new_state, new_parts)


def step_kernel(tie_row, tie_source, cols, bound_count, other, pair, ties, weights, constant, a, b, c, d,
                state, parts, new_state, new_parts, left):
    products = tie_products(tie_source, bound_count, other, pair, ties, left)
    apply_ties(tie_row, products, state, parts)
    for i in range(state.shape[0]):
        advance(i, cols[1, i], weights[i], state, parts, constant, new_state, new_parts)


def add_sums(shared, per, scenarios, i, value, sums):
    group = per * scenarios
    for k, (array, row) in enumerate(places_of(shared, per)[0]):
        piece = value[k * group : (k + 1) * group].reshape(per, scenarios, 128)
        sums[array][row : row + per, lanes(i)] = jnp.sum(piece, axis=1)


def last_step_kernel(shared, per, scenarios, tie_row, tie_source, cols, bound_count, other, pair, ties,
                     weights, constant, a, b, c, d, state, parts, new_state, new_parts, *refs):
    sums, left = refs[:-1], refs[-1]
    products = tie_products(tie_source, bound_count, other, pair, ties, left)
    apply_ties(tie_row, products, state, parts)
    for i in range(state.shape[0]):
        value = advance(i, cols[1, i], weights[i], state, parts, constant, new_state, new_parts)
        add_sums(shared, per, scenarios, i, value, sums)


def tie_products(tie_source, bound_count, other, pair, ties, left):
    for n, block in enumerate((other, pair)):
        high, low = split(block[...])
        left[n, :, 0:128] = high
        left[n, :, 128:256] = low
    partner_area = lax.axis_index("area") ^ 1
    products = []
    for m in range(ties.shape[0]):
        source = jnp.where(tie_source[m] // bound_count[0] == partner_area, 1, 0)
        product = jnp.dot(left[source], ties[m], preferred_element_type=f32)
        products.append(product[:, :128] + product[:, 128:])
    return products


def meeting(row, tie_row, products):
    total = None
    for n, product in enumerate(products):
        term = jnp.where(tie_row[n] == row, 1.0, 0.0) * product
        total = term if total is None else total + term
    return total


def apply_ties(tie_row, products, state, parts):
    count = len(products)
    values = [state[tie_row[m]] + meeting(tie_row[m], tie_row, products) for m in range(count)]
    for m in range(count):
        state[tie_row[m]] = values[m]
        store_split(parts, tie_row[m], values[m])


def boundary_after(send, other, pair, loops, state):
    value = state[send[0]]
    for n, block in enumerate((other, pair)):
        left = jnp.concatenate(split(block[...]), axis=1)
        product = jnp.dot(left, loops[n], preferred_element_type=f32)
        value = value + (product[:, :128] + product[:, 128:])
    return value


def tie_kernel(send, pair, other, loops, state, boundary):
    boundary[...] = boundary_after(send, other, pair, loops, state)


def anchor_piece(k, scen_all, scenarios, total, i):
    mean = spread(total, 0, total.shape[0], scenarios, i) * (1.0 / (scen_all >> k))
    return (step_size * penalty) * mean


def first_tie_kernel(shared, scen_all, scenarios, send, pair, other, loops, state, *refs):
    totals, boundary = refs[:shared], refs[shared]
    boundary[...] = boundary_after(send, other, pair, loops, state)
    group = totals[0].shape[0] * scenarios
    for k in range(shared):
        cut = slice(k * group, (k + 1) * group)
        boundary[cut] = boundary[cut] + anchor_piece(k, scen_all, scenarios, totals[k], send[0])


def anchor_kernel(shared, scen_all, scenarios, *refs):
    totals = refs[:shared]
    state, parts, constant = refs[shared + 3 :]
    rows = state.shape[1]
    group = totals[0].shape[0] * scenarios
    span = min(-(-shared * group // 16) * 16, rows)

    def one(i, carry):
        for k in range(shared):
            cut = slice(k * group, (k + 1) * group)
            mean = anchor_piece(k, scen_all, scenarios, totals[k], i)
            constant[i, cut] = constant[i, cut] + mean
            state[i, cut] = state[i, cut] + mean
        high_part, low_part = split(state[i, 0:span] * -step_size)
        parts[i, 0:span] = high_part
        parts[i, rows : rows + span] = low_part
        return carry

    lax.fori_loop(0, state.shape[0], one, 0, unroll=largest_divisor(state.shape[0], 14))


def last_tie_kernel(shared, per, scenarios, bound_count, tie_row, tie_source, pair, other, ties, *refs):
    left = refs[-1]
    half = (len(refs) - 1) // 2
    state, sums = refs[half], refs[half + 1 : -1]
    products = tie_products(tie_source, bound_count, other, pair, ties, left)
    count = len(products)
    values = [state[tie_row[m]] + meeting(tie_row[m], tie_row, products) for m in range(count)]
    for m in range(count):
        state[tie_row[m]] = values[m]
        add_sums(shared, per, scenarios, tie_row[m], values[m], sums)


def write_blocks(pieces, blocks, one, targets, sems):
    width = blocks // pieces
    copies = []
    for piece in range(pieces):
        lax.fori_loop(piece * width, (piece + 1) * width, one, 0, unroll=largest_divisor(width, 7))
        cut = pl.ds(piece * width * 128, width * 128)
        for buffer, out in targets:
            copies.append(pltpu.make_async_copy(buffer.at[:, :, cut], out.at[:, :, cut], sems.at[len(copies)]))
            copies[-1].start()
    for copy in copies:
        copy.wait()


def put_multipliers(chosen, scen_all, state, mult, totals, buffer, i):
    per, scenarios = buffer.shape[0] // len(chosen), buffer.shape[1]
    group = per * scenarios
    for n, k in enumerate(chosen):
        value = state[i, k * group : (k + 1) * group]
        if scen_all >> k > scenarios:
            mean = spread(totals[k], 0, per, scenarios, i) * (1.0 / (scen_all >> k))
        else:
            mean = local_mean(value, max(scen_all >> k, 1))
        gap = penalty * (value - mean)
        old = mult[k * per : (k + 1) * per, :, lanes(i)]
        buffer[n * per : (n + 1) * per, :, lanes(i)] = old + gap.reshape(per, scenarios, 128)


def output_kernel(chosen, scen_all, pieces, state, mult, dispatch, new_mult, whole, buffer, sems):
    periods, scenarios = whole.shape[:2]
    per = buffer.shape[0] // len(chosen)

    def one(i, carry):
        whole[:, :, lanes(i)] = state[i].reshape(periods, scenarios, 128)
        put_multipliers(chosen, scen_all, state, mult, {}, buffer, i)
        return carry

    rows = pl.ds(chosen[0] * per, len(chosen) * per)
    write_blocks(pieces, state.shape[0], one, [(whole, dispatch), (buffer, new_mult.at[rows])], sems)


def multiplier_kernel(chosen, scen_all, pieces, state, mult, *refs):
    new_mult, buffer, sems = refs[-3:]
    totals = dict(zip(chosen, refs[:-3]))
    per = buffer.shape[0] // len(chosen)

    def one(i, carry):
        put_multipliers(chosen, scen_all, state, mult, totals, buffer, i)
        return carry

    rows = pl.ds(chosen[0] * per, len(chosen) * per)
    write_blocks(pieces, state.shape[0], one, [(buffer, new_mult.at[rows])], sems)


def largest_divisor(count, most):
    return max(d for d in range(1, most + 1) if count % d == 0)


def local(
    start_dispatch,
    multipliers,
    demand,
    load_factor,
    node_ids,
    block_values,
    block_cols,
    send_block,
    tie_source,
    tie_row,
    tie_weight,
):
    periods, scenarios, buses = start_dispatch.shape
    blocks = buses // 128
    rows = periods * scenarios
    sections = node_ids.shape[0]
    per = periods // sections
    devices = lax.axis_size("scen")
    scen_all = scenarios * devices
    shared = devices.bit_length() - 1
    tie_count = tie_row.shape[0]

    small = [block_cols.T, tie_row, tie_source, node_ids.T, load_factor]
    padded = -(-buses // 1024) * 1024
    sum_shapes = [VMEM((size, padded if size > per else buses), f32) for size in places_of(shared, per)[1]]
    first = pl.pallas_call(
        functools.partial(first_kernel, shared, per, len(small)),
        in_specs=[smem_spec] + [any_spec] * (1 + len(small)),
        out_specs=[vmem_spec] * len(sum_shapes) + [smem_spec] * (len(small) + 1),
        out_shape=sum_shapes + [SMEM(a.shape, a.dtype) for a in small + [send_block]],
        scratch_shapes=[
            VMEM((shared * per, scenarios, buses), f32),
            pltpu.SemaphoreType.DMA((shared + len(small),)),
        ],
        compiler_params=params(4),
        cost_estimate=cost(2 * 10**10, 10**6),
        name="first_sums",
    )(send_block, in_hbm(start_dispatch), *[in_hbm(a) for a in small])
    sums = list(first[: len(sum_shapes)])
    cols, row_of_tie, source_of_tie, labels, factors, send = first[len(sum_shapes) :]

    state_shape = VMEM((blocks, rows, 128), f32)
    parts_shape = VMEM((blocks, 2 * rows, 128), bf16)

    weights_shape = VMEM((blocks, 256, 256), bf16)
    laid = {}

    def prepare(turn, totals, ready):
        after = totals[0]
        if turn == 0:
            laid["start"] = pl.pallas_call(
                functools.partial(prepare_kernel, shared, per, scen_all),
                in_specs=[smem_spec] * 5 + [vmem_spec] * 4,
                out_specs=[vmem_spec] * 7,
                out_shape=[state_shape, parts_shape, state_shape]
                + [VMEM((tie_count, 256, 256), bf16), VMEM((2, 256, 256), bf16)]
                + [VMEM((rows, 128), f32), VMEM((rows, 128), f32)],
                compiler_params=params(2),
                cost_estimate=cost(4 * 10**9, 10**6),
                name="prepare",
            )(in_smem(send), in_smem(row_of_tie), in_smem(source_of_tie), in_smem(labels), in_smem(factors),
              *[in_vmem(a) for a in (start_dispatch, multipliers, demand, tie_weight)])
            return [in_vmem(laid["start"][0])]
        if turn > 1:
            return []
        held = [in_vmem(a) for a in laid["start"][:3]]
        laid["made"] = pl.pallas_call(
            first_step_kernel,
            in_specs=[smem_spec] + [vmem_spec] * 5,
            out_specs=[vmem_spec] * 3,
            out_shape=[weights_shape, state_shape, parts_shape],
            compiler_params=params(2),
            cost_estimate=cost(10**9, 10**6),
            name="step_0",
        )(in_smem(cols), in_vmem(block_values), *held, in_vmem(after))
        return []

    totals = node_totals(sums, shared, per, buses, prepare)
    if len(turns_of(shared)) < 2:
        prepare(1, totals, [])
    spare_state, spare_parts, constant, ties, loops, load, boundary = laid["start"]
    weights, state, parts = laid["made"]
    left_shape = VMEM((2, rows, 256), bf16)
    tie_scalars = [in_smem(row_of_tie), in_smem(source_of_tie)]
    bound_count = send_block.shape[0]
    for iteration in range(STEPS):
        previous = (other, pair) if iteration > 0 else None
        other = from_other(boundary, "area")
        pair = from_pair(boundary, "area")
        if iteration > 0:
            last = iteration == STEPS - 1
            body = functools.partial(last_step_kernel, shared, per, scenarios) if last else step_kernel

            def kernel(tie_row, tie_source, cols, *refs, body=body):
                body(tie_row, tie_source, cols, (bound_count,), *refs)

            made = pl.pallas_call(
                kernel,
                in_specs=[smem_spec] * 3 + [vmem_spec] * 9,
                out_specs=[vmem_spec] * (4 + len(sum_shapes) * last),
                out_shape=[state_shape, parts_shape] * 2 + sum_shapes * last,
                input_output_aliases={8: 0, 9: 1, 10: 2, 11: 3},
                scratch_shapes=[left_shape],
                compiler_params=params(2),
                cost_estimate=cost(blocks * 2 * rows * 256 * 256 * 2, 12 * 10**6),
                name=f"step_{iteration}",
            )(*tie_scalars, in_smem(cols), *[in_vmem(a) for a in previous],
              *[in_vmem(a) for a in (ties, weights, constant, state, parts, spare_state, spare_parts)])
            spare_state, spare_parts, state, parts = made[:4]
            sums = list(made[4:])
        arrived = [in_vmem(pair), in_vmem(other)]
        if iteration < STEPS - 1:
            nodes = [in_vmem(t) for t in totals] if iteration == 0 else []
            (boundary,) = pl.pallas_call(
                functools.partial(first_tie_kernel, shared, scen_all, scenarios) if iteration == 0 else tie_kernel,
                in_specs=[smem_spec] + [vmem_spec] * (4 + len(nodes)),
                out_specs=[vmem_spec],
                out_shape=[VMEM((rows, 128), f32)],
                compiler_params=params(2),
                name=f"ties_{iteration}",
            )(in_smem(send), *arrived, in_vmem(loops), in_vmem(state), *nodes)
            if iteration == 0:
                state, parts, constant = pl.pallas_call(
                    functools.partial(anchor_kernel, shared, scen_all, scenarios),
                    in_specs=[vmem_spec] * (3 + shared),
                    out_specs=[vmem_spec] * 3,
                    out_shape=[state_shape, parts_shape, state_shape],
                    input_output_aliases={shared: 0, shared + 1: 1, shared + 2: 2},
                    compiler_params=params(2),
                    cost_estimate=cost(10**9, 10**6),
                    name="anchor",
                )(*nodes, in_vmem(state), in_vmem(parts), in_vmem(constant))
        else:
            made = pl.pallas_call(
                functools.partial(last_tie_kernel, shared, per, scenarios, (bound_count,)),
                in_specs=[smem_spec] * 2 + [vmem_spec] * (4 + len(sum_shapes)),
                out_specs=[vmem_spec] * (1 + len(sum_shapes)),
                out_shape=[state_shape] + sum_shapes,
                input_output_aliases={5 + k: k for k in range(1 + len(sum_shapes))},
                scratch_shapes=[left_shape],
                compiler_params=params(2),
                name=f"ties_{iteration}",
            )(*tie_scalars, *arrived, in_vmem(ties), in_vmem(state), *[in_vmem(a) for a in sums])
            state, sums = made[0], list(made[1:])

    state = in_vmem(state)
    pieces = largest_divisor(blocks, 5)
    written = {}

    def multiply(chosen, totals):
        extra = [in_vmem(totals[k]) for k in chosen]
        written["mult"] = pl.pallas_call(
            functools.partial(multiplier_kernel, chosen, scen_all, pieces),
            in_specs=[vmem_spec] * (2 + len(extra)) + [any_spec],
            out_specs=any_spec,
            out_shape=whole,
            input_output_aliases={2 + len(extra): 0},
            scratch_shapes=[
                VMEM((len(chosen) * per, scenarios, buses), f32),
                pltpu.SemaphoreType.DMA((pieces,)),
            ],
            compiler_params=params(5),
            cost_estimate=cost(10**9, 10**6),
            name=f"multipliers_{chosen[0]}",
        )(state, in_vmem(multipliers), *extra, in_hbm(written["mult"]))
        return [in_hbm(written["mult"])]

    open_sections = list(range(shared))
    whole = pltpu.HBM((periods, scenarios, buses), f32)

    def write(turn, totals, ready):
        if turn == 0:
            own = list(range(shared, sections))
            written["dispatch"], written["mult"] = pl.pallas_call(
                functools.partial(output_kernel, own, scen_all, pieces),
                in_specs=[vmem_spec] * 2,
                out_specs=[any_spec] * 2,
                out_shape=[whole, whole],
                scratch_shapes=[
                    VMEM((periods, scenarios, buses), f32),
                    VMEM((len(own) * per, scenarios, buses), f32),
                    pltpu.SemaphoreType.DMA((2 * pieces,)),
                ],
                compiler_params=params(8),
                cost_estimate=cost(4 * 10**9, 10**6),
                name="outputs",
            )(state, in_vmem(multipliers))
            return [in_hbm(written["dispatch"])]
        if not ready:
            return []
        for k in ready:
            open_sections.remove(k)
        return multiply(ready, totals)

    totals = node_totals(sums, shared, per, buses, write)
    dispatch = written["dispatch"]
    new_mult = multiply(open_sections, totals)[0]
    return dispatch, new_mult


def solution(mesh):
    in_specs = (
        P(None, "scen", "area"),
        P(None, "scen", "area"),
        P(None, "area"),
        P(),
        P(None, "scen"),
        P("area", None, None, None),
        P("area", None),
        P("area"),
        P("area"),
        P("area"),
        P("area", None, None),
    )
    out_specs = (P(None, "scen", "area"), P(None, "scen", "area"))
    return jax.shard_map(local, mesh=mesh, in_specs=in_specs, out_specs=out_specs, check_vma=False)
```

```python
import functools

import jax
import jax.numpy as jnp
from jax import lax
from jax.experimental import pallas as pl
from jax.experimental.pallas import tpu as pltpu
from jax.sharding import PartitionSpec as P

STEPS = 8
step_size = 0.25
penalty = 1.0
keep = 1.0 - step_size * penalty

f32 = jnp.float32
bf16 = jnp.bfloat16
VMEM = pltpu.VMEM
SMEM = pltpu.SMEM
MIB = 1 << 20


def in_vmem(array):
    return pltpu.with_memory_space_constraint(array, VMEM)


def in_smem(array):
    return pltpu.with_memory_space_constraint(array, SMEM)


def in_hbm(array):
    return pltpu.with_memory_space_constraint(array, pltpu.HBM)


vmem_spec = pl.BlockSpec(memory_space=VMEM)
smem_spec = pl.BlockSpec(memory_space=SMEM)
any_spec = pl.BlockSpec(memory_space=pl.ANY)


def params(mib):
    return pltpu.CompilerParams(vmem_limit_bytes=mib * MIB)


def cost(flops, moved):
    return pl.CostEstimate(flops=flops, bytes_accessed=moved, transcendentals=0)


def split(value):
    high = value.astype(bf16)
    return high, (value - high.astype(f32)).astype(bf16)


def store_split(ref, index, value):
    rows = value.shape[0]
    high, low = split(value)
    ref[index, 0:rows] = high
    ref[index, rows : 2 * rows] = low


def fold(product, rows):
    return (product[:rows, :128] + product[:rows, 128:]) + (product[rows:, :128] + product[rows:, 128:])


def lanes(block):
    return pl.ds(pl.multiple_of(block * 128, 128), 128)


def partner(value, apart):
    rows = value.shape[0]
    up = pltpu.roll(value, rows - apart, 0)
    down = pltpu.roll(value, apart, 0)
    place = lax.broadcasted_iota(jnp.int32, value.shape, 0)
    return jnp.where((place & apart) == 0, up, down)


def local_mean(value, members):
    total, apart = value, 1
    while apart < members:
        total = total + partner(total, apart)
        apart *= 2
    return total * (1.0 / members)


def spread(ref, first, count, scenarios, block):
    shape = (count * scenarios, 128)
    place = lax.broadcasted_iota(jnp.int32, shape, 0)
    wide = jnp.broadcast_to(ref[first : first + 1, lanes(block)], shape)
    for t in range(1, count):
        row = jnp.broadcast_to(ref[first + t : first + t + 1, lanes(block)], shape)
        wide = jnp.where(place < t * scenarios, wide, row)
    return wide


def copies_of(pairs, sems):
    copies = [pltpu.make_async_copy(source, target, sems.at[n]) for n, (source, target) in enumerate(pairs)]
    for copy in copies:
        copy.start()
    return copies


def first_kernel(shared, per, small, send, start, *refs):
    sources, refs = refs[:small], refs[small:]
    places, sizes = places_of(shared, per)
    sums, targets = refs[: len(sizes)], refs[len(sizes) : len(sizes) + small]
    send_out, head, sems = refs[len(sizes) + small :]
    cuts = [pl.ds(k * per, per) for k in range(shared)]
    pairs = [(start.at[cut], head.at[cut]) for cut in cuts] + list(zip(sources, targets))
    copies = copies_of(pairs, sems)
    for k in range(shared):
        copies[k].wait()
        array, row = places[k]
        sums[array][row : row + per, 0 : head.shape[2]] = jnp.sum(head[k * per : (k + 1) * per], axis=1)
    send_out[0] = send[0]
    for copy in copies[shared:]:
        copy.wait()


def turns_of(levels):
    if levels < 3:
        return [[1 << level] for level in range(levels)]
    low = 1 << (levels - 2)
    return [[low, 2 * low, 3 * low]] + turns_of(levels - 2)


def swap(block, axis, apart):
    count = lax.axis_size(axis)
    return lax.ppermute(block, axis, [(i, i ^ apart) for i in range(count)])


def places_of(shared, per):
    groups, places, sizes = {}, [], []
    for k in range(shared):
        key = tuple(turns_of(shared - k)[0])
        if key not in groups:
            groups[key] = len(sizes)
            sizes.append(0)
        places.append((groups[key], sizes[groups[key]]))
        sizes[groups[key]] += per
    return places, sizes


def add_kernel(cuts, counts, *refs):
    inputs, outputs = iter(refs), refs[-len(counts) :]
    for cut, count, output in zip(cuts, counts, outputs):
        wide = slice(0, output.shape[1])
        total = next(inputs)[cut, wide]
        for _ in range(count):
            total = total + next(inputs)[cut, wide]
        output[...] = total


def node_totals(sums, shared, per, buses, beside):
    places, sizes = places_of(shared, per)
    totals = [sums[places[k][0]] for k in range(shared)]
    plans = [turns_of(shared - k) for k in range(shared)]
    for turn in range(max(len(plan) for plan in plans)):
        active = [k for k in range(shared) if turn < len(plans[k])]
        operands, cuts, received = [], [], {}
        for k in active:
            key = places[k][0] if turn == 0 else shared + k
            if key not in received:
                received[key] = [swap(totals[k], "scen", apart) for apart in plans[k][turn]]
            operands += [totals[k]] + received[key]
            cuts.append(slice(places[k][1], places[k][1] + per) if turn == 0 else slice(0, per))
        after = beside(turn, totals, [k for k in range(shared) if len(plans[k]) == turn])
        counts = [len(plans[k][turn]) for k in active]
        added = pl.pallas_call(
            functools.partial(add_kernel, cuts, counts),
            in_specs=[vmem_spec] * len(operands) + [any_spec] * len(after),
            out_specs=[vmem_spec] * len(active),
            out_shape=[VMEM((per, buses), f32) for k in active],
            compiler_params=params(2),
            name=f"node_add_{turn}",
        )(*[in_vmem(a) for a in operands], *after)
        for k, value in zip(active, added):
            totals[k] = value
    return totals


def from_pair(value, axis):
    count = lax.axis_size(axis)
    return lax.ppermute(value, axis, [(i, i ^ 1) for i in range(count)])


def from_other(value, axis):
    count = lax.axis_size(axis)
    return lax.ppermute(value, axis, [(i, (i + 1 if i % 2 else i - 1) % count) for i in range(count)])


def prepare_kernel(shared, per, scen_all, send, tie_row, tie_source, node_ids, load_factor,
                   start, mult, demand, tie_weight, state, parts, constant, ties, loops, load, boundary):
    rows = state.shape[1]
    scenarios = start.shape[1]
    group = per * scenarios
    for k in range(node_ids.shape[1]):
        for s in range(scenarios):
            row = jnp.full((1, 128), load_factor[node_ids[s, k]], f32)
            for t in range(per):
                at = (k * per + t) * scenarios + s
                load[at : at + 1] = row
    boundary[...] = start[:, :, lanes(send[0])].reshape(boundary.shape)
    def put_matrix(ref, n, value):
        high, low = split(value)
        for half in range(2):
            ref[n, half * 128 : (half + 1) * 128, 0:128] = high
            ref[n, half * 128 : (half + 1) * 128, 128:256] = low

    partner_area = lax.axis_index("area") ^ 1
    ending = [jnp.zeros((128, 128), f32)] * 2
    for m in range(tie_weight.shape[0]):
        value = tie_weight[m] * -step_size
        put_matrix(ties, m, value)
        ends = tie_row[m] == send[0]
        paired = tie_source[m] // send.shape[0] == partner_area
        ending[0] = ending[0] + jnp.where(jnp.logical_and(ends, jnp.logical_not(paired)), 1.0, 0.0) * value
        ending[1] = ending[1] + jnp.where(jnp.logical_and(ends, paired), 1.0, 0.0) * value
    for n in range(2):
        put_matrix(loops, n, ending[n])

    def one(i, carry):
        for k in range(rows // group):
            cut = slice(k * group, (k + 1) * group)
            span = slice(k * per, (k + 1) * per)
            x = start[span, :, lanes(i)].reshape(group, 128)
            m = mult[span, :, lanes(i)].reshape(group, 128)
            rest = m - spread(demand, k * per, per, scenarios, i) * load[cut]
            if k >= shared:
                rest = rest - penalty * local_mean(x, max(scen_all >> k, 1))
            constant[i, cut] = -step_size * rest
            state[i, cut] = x
        store_split(parts, i, state[i])
        return carry

    lax.fori_loop(0, state.shape[0], one, 0, unroll=largest_divisor(state.shape[0], 7))


def advance(i, other, weight, state, parts, constant, new_state, new_parts):
    left = jnp.concatenate([parts[i], parts[other]], axis=1)
    product = jnp.dot(left, weight, preferred_element_type=f32)
    value = (keep * state[i] + constant[i]) + fold(product, state.shape[1])
    new_state[i] = value
    store_split(new_parts, i, value)
    return value


def first_step_kernel(cols, values, state, parts, constant, after, weights, new_state, new_parts):
    for i in range(state.shape[0]):
        weight = jnp.concatenate([jnp.concatenate(split(values[i, j] * -step_size), axis=1) for j in range(2)], axis=0)
        weights[i] = weight
        advance(i, cols[1, i], weight, state, parts, constant, new_state, new_parts)


def step_kernel(tie_row, tie_source, cols, bound_count, other, pair, ties, weights, constant, a, b, c, d,
                state, parts, new_state, new_parts, left):
    products = tie_products(tie_source, bound_count, other, pair, ties, left)
    apply_ties(tie_row, products, state, parts)
    for i in range(state.shape[0]):
        advance(i, cols[1, i], weights[i], state, parts, constant, new_state, new_parts)


def add_sums(shared, per, scenarios, i, value, sums):
    group = per * scenarios
    for k, (array, row) in enumerate(places_of(shared, per)[0]):
        piece = value[k * group : (k + 1) * group].reshape(per, scenarios, 128)
        sums[array][row : row + per, lanes(i)] = jnp.sum(piece, axis=1)


def last_step_kernel(shared, per, scenarios, tie_row, tie_source, cols, bound_count, other, pair, ties,
                     weights, constant, a, b, c, d, state, parts, new_state, new_parts, *refs):
    sums, left = refs[:-1], refs[-1]
    products = tie_products(tie_source, bound_count, other, pair, ties, left)
    apply_ties(tie_row, products, state, parts)
    for i in range(state.shape[0]):
        value = advance(i, cols[1, i], weights[i], state, parts, constant, new_state, new_parts)
        add_sums(shared, per, scenarios, i, value, sums)


def tie_products(tie_source, bound_count, other, pair, ties, left):
    for n, block in enumerate((other, pair)):
        high, low = split(block[...])
        left[n, :, 0:128] = high
        left[n, :, 128:256] = low
    partner_area = lax.axis_index("area") ^ 1
    products = []
    for m in range(ties.shape[0]):
        source = jnp.where(tie_source[m] // bound_count[0] == partner_area, 1, 0)
        product = jnp.dot(left[source], ties[m], preferred_element_type=f32)
        products.append(product[:, :128] + product[:, 128:])
    return products


def meeting(row, tie_row, products):
    total = None
    for n, product in enumerate(products):
        term = jnp.where(tie_row[n] == row, 1.0, 0.0) * product
        total = term if total is None else total + term
    return total


def apply_ties(tie_row, products, state, parts):
    count = len(products)
    values = [state[tie_row[m]] + meeting(tie_row[m], tie_row, products) for m in range(count)]
    for m in range(count):
        state[tie_row[m]] = values[m]
        store_split(parts, tie_row[m], values[m])


def boundary_after(send, other, pair, loops, state):
    value = state[send[0]]
    for n, block in enumerate((other, pair)):
        left = jnp.concatenate(split(block[...]), axis=1)
        product = jnp.dot(left, loops[n], preferred_element_type=f32)
        value = value + (product[:, :128] + product[:, 128:])
    return value


def tie_kernel(send, pair, other, loops, state, boundary):
    boundary[...] = boundary_after(send, other, pair, loops, state)


def anchor_piece(k, scen_all, scenarios, total, i):
    mean = spread(total, 0, total.shape[0], scenarios, i) * (1.0 / (scen_all >> k))
    return (step_size * penalty) * mean


def first_tie_kernel(shared, scen_all, scenarios, send, pair, other, loops, state, *refs):
    totals, boundary = refs[:shared], refs[shared]
    boundary[...] = boundary_after(send, other, pair, loops, state)
    group = totals[0].shape[0] * scenarios
    for k in range(shared):
        cut = slice(k * group, (k + 1) * group)
        boundary[cut] = boundary[cut] + anchor_piece(k, scen_all, scenarios, totals[k], send[0])


def anchor_kernel(shared, scen_all, scenarios, *refs):
    totals = refs[:shared]
    state, parts, constant = refs[shared + 3 :]
    rows = state.shape[1]
    group = totals[0].shape[0] * scenarios
    span = min(-(-shared * group // 16) * 16, rows)

    def one(i, carry):
        for k in range(shared):
            cut = slice(k * group, (k + 1) * group)
            mean = anchor_piece(k, scen_all, scenarios, totals[k], i)
            constant[i, cut] = constant[i, cut] + mean
            state[i, cut] = state[i, cut] + mean
        high_part, low_part = split(state[i, 0:span])
        parts[i, 0:span] = high_part
        parts[i, rows : rows + span] = low_part
        return carry

    lax.fori_loop(0, state.shape[0], one, 0, unroll=largest_divisor(state.shape[0], 14))


def last_tie_kernel(shared, per, scenarios, bound_count, tie_row, tie_source, pair, other, ties, *refs):
    left = refs[-1]
    half = (len(refs) - 1) // 2
    state, sums = refs[half], refs[half + 1 : -1]
    products = tie_products(tie_source, bound_count, other, pair, ties, left)
    count = len(products)
    values = [state[tie_row[m]] + meeting(tie_row[m], tie_row, products) for m in range(count)]
    for m in range(count):
        state[tie_row[m]] = values[m]
        add_sums(shared, per, scenarios, tie_row[m], values[m], sums)


def write_blocks(pieces, blocks, one, targets, sems):
    width = blocks // pieces
    copies = []
    for piece in range(pieces):
        lax.fori_loop(piece * width, (piece + 1) * width, one, 0, unroll=largest_divisor(width, 7))
        cut = pl.ds(piece * width * 128, width * 128)
        for buffer, out in targets:
            copies.append(pltpu.make_async_copy(buffer.at[:, :, cut], out.at[:, :, cut], sems.at[len(copies)]))
            copies[-1].start()
    for copy in copies:
        copy.wait()


def put_multipliers(chosen, scen_all, state, mult, totals, buffer, i):
    per, scenarios = buffer.shape[0] // len(chosen), buffer.shape[1]
    group = per * scenarios
    for n, k in enumerate(chosen):
        value = state[i, k * group : (k + 1) * group]
        if scen_all >> k > scenarios:
            mean = spread(totals[k], 0, per, scenarios, i) * (1.0 / (scen_all >> k))
        else:
            mean = local_mean(value, max(scen_all >> k, 1))
        gap = penalty * (value - mean)
        old = mult[k * per : (k + 1) * per, :, lanes(i)]
        buffer[n * per : (n + 1) * per, :, lanes(i)] = old + gap.reshape(per, scenarios, 128)


def output_kernel(chosen, scen_all, pieces, state, mult, dispatch, new_mult, whole, buffer, sems):
    periods, scenarios = whole.shape[:2]
    per = buffer.shape[0] // len(chosen)

    def one(i, carry):
        whole[:, :, lanes(i)] = state[i].reshape(periods, scenarios, 128)
        put_multipliers(chosen, scen_all, state, mult, {}, buffer, i)
        return carry

    rows = pl.ds(chosen[0] * per, len(chosen) * per)
    write_blocks(pieces, state.shape[0], one, [(whole, dispatch), (buffer, new_mult.at[rows])], sems)


def multiplier_kernel(chosen, scen_all, pieces, state, mult, *refs):
    new_mult, buffer, sems = refs[-3:]
    totals = dict(zip(chosen, refs[:-3]))
    per = buffer.shape[0] // len(chosen)

    def one(i, carry):
        put_multipliers(chosen, scen_all, state, mult, totals, buffer, i)
        return carry

    rows = pl.ds(chosen[0] * per, len(chosen) * per)
    write_blocks(pieces, state.shape[0], one, [(buffer, new_mult.at[rows])], sems)


def largest_divisor(count, most):
    return max(d for d in range(1, most + 1) if count % d == 0)


def local(
    start_dispatch,
    multipliers,
    demand,
    load_factor,
    node_ids,
    block_values,
    block_cols,
    send_block,
    tie_source,
    tie_row,
    tie_weight,
):
    periods, scenarios, buses = start_dispatch.shape
    blocks = buses // 128
    rows = periods * scenarios
    sections = node_ids.shape[0]
    per = periods // sections
    devices = lax.axis_size("scen")
    scen_all = scenarios * devices
    shared = devices.bit_length() - 1
    tie_count = tie_row.shape[0]

    small = [block_cols.T, tie_row, tie_source, node_ids.T, load_factor]
    padded = -(-buses // 1024) * 1024
    sum_shapes = [VMEM((size, padded if size > per else buses), f32) for size in places_of(shared, per)[1]]
    first = pl.pallas_call(
        functools.partial(first_kernel, shared, per, len(small)),
        in_specs=[smem_spec] + [any_spec] * (1 + len(small)),
        out_specs=[vmem_spec] * len(sum_shapes) + [smem_spec] * (len(small) + 1),
        out_shape=sum_shapes + [SMEM(a.shape, a.dtype) for a in small + [send_block]],
        scratch_shapes=[
            VMEM((shared * per, scenarios, buses), f32),
            pltpu.SemaphoreType.DMA((shared + len(small),)),
        ],
        compiler_params=params(4),
        cost_estimate=cost(2 * 10**10, 10**6),
        name="first_sums",
    )(send_block, in_hbm(start_dispatch), *[in_hbm(a) for a in small])
    sums = list(first[: len(sum_shapes)])
    cols, row_of_tie, source_of_tie, labels, factors, send = first[len(sum_shapes) :]

    state_shape = VMEM((blocks, rows, 128), f32)
    parts_shape = VMEM((blocks, 2 * rows, 128), bf16)

    weights_shape = VMEM((blocks, 256, 256), bf16)
    laid = {}

    def prepare(turn, totals, ready):
        after = totals[0]
        if turn == 0:
            laid["start"] = pl.pallas_call(
                functools.partial(prepare_kernel, shared, per, scen_all),
                in_specs=[smem_spec] * 5 + [vmem_spec] * 4,
                out_specs=[vmem_spec] * 7,
                out_shape=[state_shape, parts_shape, state_shape]
                + [VMEM((tie_count, 256, 256), bf16), VMEM((2, 256, 256), bf16)]
                + [VMEM((rows, 128), f32), VMEM((rows, 128), f32)],
                compiler_params=params(2),
                cost_estimate=cost(4 * 10**9, 10**6),
                name="prepare",
            )(in_smem(send), in_smem(row_of_tie), in_smem(source_of_tie), in_smem(labels), in_smem(factors),
              *[in_vmem(a) for a in (start_dispatch, multipliers, demand, tie_weight)])
            return [in_vmem(laid["start"][0])]
        if turn > 1:
            return []
        held = [in_vmem(a) for a in laid["start"][:3]]
        laid["made"] = pl.pallas_call(
            first_step_kernel,
            in_specs=[smem_spec] + [vmem_spec] * 5,
            out_specs=[vmem_spec] * 3,
            out_shape=[weights_shape, state_shape, parts_shape],
            compiler_params=params(2),
            cost_estimate=cost(10**9, 10**6),
            name="step_0",
        )(in_smem(cols), in_vmem(block_values), *held, in_vmem(after))
        return []

    totals = node_totals(sums, shared, per, buses, prepare)
    if len(turns_of(shared)) < 2:
        prepare(1, totals, [])
    spare_state, spare_parts, constant, ties, loops, load, boundary = laid["start"]
    weights, state, parts = laid["made"]
    left_shape = VMEM((2, rows, 256), bf16)
    tie_scalars = [in_smem(row_of_tie), in_smem(source_of_tie)]
    bound_count = send_block.shape[0]
    for iteration in range(STEPS):
        previous = (other, pair) if iteration > 0 else None
        other = from_other(boundary, "area")
        pair = from_pair(boundary, "area")
        if iteration > 0:
            last = iteration == STEPS - 1
            body = functools.partial(last_step_kernel, shared, per, scenarios) if last else step_kernel

            def kernel(tie_row, tie_source, cols, *refs, body=body):
                body(tie_row, tie_source, cols, (bound_count,), *refs)

            made = pl.pallas_call(
                kernel,
                in_specs=[smem_spec] * 3 + [vmem_spec] * 9,
                out_specs=[vmem_spec] * (4 + len(sum_shapes) * last),
                out_shape=[state_shape, parts_shape] * 2 + sum_shapes * last,
                input_output_aliases={8: 0, 9: 1, 10: 2, 11: 3},
                scratch_shapes=[left_shape],
                compiler_params=params(2),
                cost_estimate=cost(blocks * 2 * rows * 256 * 256 * 2, 12 * 10**6),
                name="last_step" if last else "step",
            )(*tie_scalars, in_smem(cols), *[in_vmem(a) for a in previous],
              *[in_vmem(a) for a in (ties, weights, constant, state, parts, spare_state, spare_parts)])
            spare_state, spare_parts, state, parts = made[:4]
            sums = list(made[4:])
        arrived = [in_vmem(pair), in_vmem(other)]
        if iteration < STEPS - 1:
            nodes = [in_vmem(t) for t in totals] if iteration == 0 else []
            (boundary,) = pl.pallas_call(
                functools.partial(first_tie_kernel, shared, scen_all, scenarios) if iteration == 0 else tie_kernel,
                in_specs=[smem_spec] + [vmem_spec] * (4 + len(nodes)),
                out_specs=[vmem_spec],
                out_shape=[VMEM((rows, 128), f32)],
                compiler_params=params(2),
                name="first_ties" if iteration == 0 else "ties",
            )(in_smem(send), *arrived, in_vmem(loops), in_vmem(state), *nodes)
            if iteration == 0:
                state, parts, constant = pl.pallas_call(
                    functools.partial(anchor_kernel, shared, scen_all, scenarios),
                    in_specs=[vmem_spec] * (3 + shared),
                    out_specs=[vmem_spec] * 3,
                    out_shape=[state_shape, parts_shape, state_shape],
                    input_output_aliases={shared: 0, shared + 1: 1, shared + 2: 2},
                    compiler_params=params(2),
                    cost_estimate=cost(10**9, 10**6),
                    name="anchor",
                )(*nodes, in_vmem(state), in_vmem(parts), in_vmem(constant))
        else:
            made = pl.pallas_call(
                functools.partial(last_tie_kernel, shared, per, scenarios, (bound_count,)),
                in_specs=[smem_spec] * 2 + [vmem_spec] * (4 + len(sum_shapes)),
                out_specs=[vmem_spec] * (1 + len(sum_shapes)),
                out_shape=[state_shape] + sum_shapes,
                input_output_aliases={5 + k: k for k in range(1 + len(sum_shapes))},
                scratch_shapes=[left_shape],
                compiler_params=params(2),
                name="last_ties",
            )(*tie_scalars, *arrived, in_vmem(ties), in_vmem(state), *[in_vmem(a) for a in sums])
            state, sums = made[0], list(made[1:])

    state = in_vmem(state)
    pieces = largest_divisor(blocks, 5)
    written = {}

    def multiply(chosen, totals):
        extra = [in_vmem(totals[k]) for k in chosen]
        written["mult"] = pl.pallas_call(
            functools.partial(multiplier_kernel, chosen, scen_all, pieces),
            in_specs=[vmem_spec] * (2 + len(extra)) + [any_spec],
            out_specs=any_spec,
            out_shape=whole,
            input_output_aliases={2 + len(extra): 0},
            scratch_shapes=[
                VMEM((len(chosen) * per, scenarios, buses), f32),
                pltpu.SemaphoreType.DMA((pieces,)),
            ],
            compiler_params=params(5),
            cost_estimate=cost(10**9, 10**6),
            name=f"multipliers_{chosen[0]}",
        )(state, in_vmem(multipliers), *extra, in_hbm(written["mult"]))
        return [in_hbm(written["mult"])]

    open_sections = list(range(shared))
    whole = pltpu.HBM((periods, scenarios, buses), f32)

    def write(turn, totals, ready):
        if turn == 0:
            own = list(range(shared, sections))
            written["dispatch"], written["mult"] = pl.pallas_call(
                functools.partial(output_kernel, own, scen_all, pieces),
                in_specs=[vmem_spec] * 2,
                out_specs=[any_spec] * 2,
                out_shape=[whole, whole],
                scratch_shapes=[
                    VMEM((periods, scenarios, buses), f32),
                    VMEM((len(own) * per, scenarios, buses), f32),
                    pltpu.SemaphoreType.DMA((2 * pieces,)),
                ],
                compiler_params=params(8),
                cost_estimate=cost(4 * 10**9, 10**6),
                name="outputs",
            )(state, in_vmem(multipliers))
            return [in_hbm(written["dispatch"])]
        if not ready:
            return []
        for k in ready:
            open_sections.remove(k)
        return multiply(ready, totals)

    totals = node_totals(sums, shared, per, buses, write)
    dispatch = written["dispatch"]
    new_mult = multiply(open_sections, totals)[0]
    return dispatch, new_mult


def solution(mesh):
    in_specs = (
        P(None, "scen", "area"),
        P(None, "scen", "area"),
        P(None, "area"),
        P(),
        P(None, "scen"),
        P("area", None, None, None),
        P("area", None),
        P("area"),
        P("area"),
        P("area"),
        P("area", None, None),
    )
    out_specs = (P(None, "scen", "area"), P(None, "scen", "area"))
    return jax.shard_map(local, mesh=mesh, in_specs=in_specs, out_specs=out_specs, check_vma=False)
```
